512 devices in a mesh: tm: 32 (over z_lo, y, core), rows: 16 (over z_hi, x).
Axes of the slice: x: 4, y: 4, z: 16 (z_hi: 4, z_lo: 4; z = z_hi * 4 + z_lo), core: 2. Of those that a mesh axis runs over, the one named last changes fastest.
Arguments:
- video: bfloat16 [64, 64, 120, 128], P('tm', 'rows'), may hold values from -6 to 6
- norm_gain: bfloat16 [128], replicated, may hold values from 0.099609375 to 1.8984375
- conv_first: bfloat16 [3, 3, 3, 128, 128], replicated, may hold values from -0.109375 to 0.109375
- conv_second: bfloat16 [3, 3, 3, 128, 128], replicated, may hold values from -0.109375 to 0.109375
- attn_gain: bfloat16 [128], replicated, may hold values from 0.099609375 to 1.8984375
- query_weight: bfloat16 [128, 128], replicated, may hold values from -2 to 2
- key_weight: bfloat16 [128, 128], replicated, may hold values from -2 to 2
- value_weight: bfloat16 [128, 128], replicated, may hold values from -0.5 to 0.5
- out_weight: bfloat16 [128, 128], replicated, may hold values from -0.5 to 0.5
Outputs:
- result: bfloat16 [64, 64, 120, 128], P('tm', 'rows')
The draws below stay inside these ranges and needn't reach their ends.
All inputs are finite; a program needn't handle non-finite values.
Results may differ from the reference program's by a relative error of at most 0.013.
Values may be sent and summed in bfloat16 or wider, within the bound.
A program may use at most 64 MiB of HBM per device.

```python
import jax
import jax.numpy as jnp
from jax import lax

C = 128
W = 120
FRAMES = 64
HEIGHT = 64


def shared_base(key):
    return jnp.clip(jax.random.normal(jax.random.fold_in(key, 11), (C, C), jnp.float32), -4.0, 4.0)


def draw_query_weight(key, part):
    base = shared_base(key)
    scaled = base * C ** (-0.5)
    return jnp.clip(scaled, -2.0, 2.0).astype(jnp.bfloat16)


def draw_key_weight(key, part):
    other = jnp.clip(jax.random.normal(jax.random.fold_in(key, 13), (C, C), jnp.float32), -4.0, 4.0)
    scaled = other * C ** (-0.5)
    return jnp.clip(scaled, -2.0, 2.0).astype(jnp.bfloat16)


def block_scale(stream_key, extent, cuts, least, largest):
    level, own = 1.0, jax.random.fold_in(stream_key, 6)
    for dim, blocks in cuts:
        draws = jnp.exp(jax.random.uniform(jax.random.fold_in(own, dim), (blocks,), jnp.float32, least / len(cuts), largest / len(cuts)))
        level = level * jnp.repeat(draws, extent[dim] // blocks).reshape([-1 if axis == dim else 1 for axis in range(len(extent))])
    return level


def gaussian(own_key, shape, scale, limit, shards=(), held_as=jnp.bfloat16):
    entries = scale * jax.random.normal(own_key, shape, jnp.float32)
    if shards:
        entries = entries * block_scale(own_key, shape, shards, -0.22, 0.18)
    return jnp.clip(entries, -limit, limit).astype(held_as)


def setup_inputs(seed: int = 0) -> dict:
    arg_keys = jax.random.split(jax.random.key(seed), 10)
    video = gaussian(arg_keys[0], (FRAMES, HEIGHT, W, C), 1.0, 6.0, ((0, 32), (1, 16)))
    norm_gain = jnp.clip(1.0 + 0.18 * jax.random.normal(arg_keys[1], (C,), jnp.float32), 0.099609375, 1.8984375).astype(jnp.bfloat16)
    conv_first = gaussian(arg_keys[2], (3, 3, 3, C, C), (27 * C) ** -0.5, 0.109375)
    conv_second = gaussian(arg_keys[3], (3, 3, 3, C, C), (27 * C) ** -0.5, 0.109375)
    attn_gain = jnp.clip(1.0 + 0.18 * jax.random.normal(arg_keys[4], (C,), jnp.float32), 0.099609375, 1.8984375).astype(jnp.bfloat16)
    query_weight = draw_query_weight(jax.random.fold_in(arg_keys[9], 71), 0)
    key_weight = draw_key_weight(jax.random.fold_in(arg_keys[9], 71), 0)
    value_weight = gaussian(arg_keys[7], (C, C), C ** -0.5, 0.5)
    out_weight = gaussian(arg_keys[8], (C, C), C ** -0.5, 0.5)
    return {"video": video, "norm_gain": norm_gain, "conv_first": conv_first, "conv_second": conv_second, "attn_gain": attn_gain, "query_weight": query_weight, "key_weight": key_weight, "value_weight": value_weight, "out_weight": out_weight}


def rms_norm(values, gain):
    wide = values.astype(jnp.float32)
    scale = lax.rsqrt(lax.optimization_barrier(jnp.mean(wide * wide, axis=-1, keepdims=True)) + 1e-06)
    return wide * scale * gain.astype(jnp.float32)

def conv_taps(padded, kernel, frames, height, width):
    chans = kernel.shape[-1]
    total = jnp.zeros((frames * height * width, chans), jnp.float32)
    for shift_t in range(3):
        for shift_h in range(3):
            slab = padded[shift_t:shift_t + frames, shift_h:shift_h + height]
            joined = jnp.concatenate([slab[:, :, e:e + width] for e in range(3)], axis=-1)
            taps = kernel[shift_t, shift_h].reshape(3 * chans, chans)
            total = total + jnp.dot(joined.reshape(-1, 3 * chans), taps, preferred_element_type=jnp.float32)
    return total.reshape(frames, height, width, chans)

def convolve(field, kernel):
    frames, height, width, chans = field.shape
    padded = jnp.pad(field, ((2, 0), (1, 1), (1, 1), (0, 0)))
    return conv_taps(padded, kernel, frames, height, width)

def reference(video, norm_gain, conv_first, conv_second, attn_gain, query_weight, key_weight, value_weight, out_weight):
    frames, height, width, chans = video.shape
    act = jax.nn.silu(rms_norm(video, norm_gain)).astype(jnp.bfloat16)
    mid = jax.nn.silu(convolve(act, conv_first)).astype(jnp.bfloat16)
    hidden = (video.astype(jnp.float32) + convolve(mid, conv_second)).astype(jnp.bfloat16)
    normed = rms_norm(hidden, attn_gain).astype(jnp.bfloat16)
    flat = normed.reshape(-1, chans)
    query = jnp.dot(flat, query_weight, preferred_element_type=jnp.float32).astype(jnp.bfloat16)
    keys = jnp.dot(flat, key_weight, preferred_element_type=jnp.float32).astype(jnp.bfloat16)
    values = jnp.dot(flat, value_weight, preferred_element_type=jnp.float32).astype(jnp.bfloat16)
    cells = height * width
    query = query.reshape(frames, cells, chans).astype(jnp.float32)
    keys = keys.reshape(frames, cells, chans).astype(jnp.float32)
    values = values.reshape(frames, cells, chans).astype(jnp.float32)
    scores = jnp.einsum('fpc,gpc->fgp', query, keys) / jnp.sqrt(jnp.float32(chans))
    position = jnp.arange(frames, dtype=jnp.int32)
    allowed = (position[None, :] <= position[:, None])[:, :, None]
    top = lax.optimization_barrier(jnp.max(jnp.where(allowed, scores, jnp.float32(-1e+30)), axis=1))
    weights = jnp.where(allowed, jnp.exp(scores - top[:, None, :]), jnp.float32(0.0))
    total = lax.optimization_barrier(jnp.sum(weights, axis=1))
    acc = jnp.einsum('fgp,gpc->fpc', weights.astype(jnp.bfloat16).astype(jnp.float32), values)
    mixed = (acc / total[:, :, None]).astype(jnp.bfloat16)
    projected = jnp.dot(mixed.reshape(-1, chans), out_weight, preferred_element_type=jnp.float32)
    result = hidden.reshape(-1, chans).astype(jnp.float32) + projected
    return result.astype(jnp.bfloat16).reshape(frames, height, width, chans)
```

```python
import functools

import jax
import jax.numpy as jnp
from jax import lax
from jax.experimental import pallas as pl
from jax.experimental.pallas import tpu as pltpu
from jax.sharding import PartitionSpec as P

F32 = jnp.float32
BF16 = jnp.bfloat16
MESH = pl.DeviceIdType.MESH
COLS = 128
UNIT = 8
PER_ROW = COLS // UNIT


def rms_norm(wide, gain):
    scale = lax.rsqrt(jnp.mean(wide * wide, axis=-1, keepdims=True) + 1e-06)
    return wide * scale * gain


def silu(v):
    return v / (1.0 + jnp.exp(-v))


def column_sum(total):
    width, chans = (COLS - UNIT, total.shape[1] // 3)
    left = pltpu.roll(total[:, :chans], 1, 0)
    right = pltpu.roll(total[:, 2 * chans :], COLS - 1, 0)
    return (left + total[:, chans : 2 * chans] + right)[:width]


def padded(value):
    return jnp.concatenate([value, jnp.zeros((COLS - value.shape[0], value.shape[1]), F32)], axis=0)


def taps_of(weight, pairs):
    return jnp.concatenate(
        [jnp.concatenate([weight[a, b, e] for e in range(3)], axis=1) for a, b in pairs], axis=0
    )


def cells_of(field, frame, pairs, rows):
    return jnp.concatenate(
        [
            jnp.concatenate([field[frame + a, row + b] for row in rows], axis=0)
            for a, b in pairs
        ],
        axis=1,
    )


def kernel(
    steps,
    blocks,
    video_hbm,
    norm_gain_hbm,
    first_hbm,
    second_hbm,
    attn_gain_hbm,
    query_hbm,
    key_hbm,
    value_hbm,
    out_hbm,
    result_ref,
    video,
    norm_gain,
    first,
    second,
    attn_gain,
    query_w,
    key_w,
    value_w,
    out_w,
    act,
    mid,
    acc,
    hidden,
    gathered,
    answer,
    returned,
    load_sem,
    halo_send,
    halo_recv,
    swap_send,
    swap_recv,
):
    t, r = (lax.axis_index("tm"), lax.axis_index("rows"))
    chans = video.shape[-1]
    loads = [
        pltpu.make_async_copy(src, dst, load_sem.at[i])
        for i, (src, dst) in enumerate(
            [
                (video_hbm, video),
                (norm_gain_hbm, norm_gain),
                (first_hbm, first),
                (second_hbm, second),
                (attn_gain_hbm, attn_gain),
                (query_hbm, query_w),
                (key_hbm, key_w),
                (value_hbm, value_w),
                (out_hbm, out_w),
            ]
        )
    ]
    for load in loads:
        load.start()

    has_next, has_prev = (t < steps - 1, t > 0)
    has_above, has_below = (r < blocks - 1, r > 0)

    barrier = pltpu.get_barrier_semaphore()

    def greet(j, _):
        peer = lax.rem(t + j, steps)
        pl.semaphore_signal(barrier, inc=1, device_id={"tm": peer, "rows": r}, device_id_type=MESH)
        return 0

    lax.fori_loop(1, steps, greet, 0)

    @pl.when(has_above)
    def _():
        pl.semaphore_signal(barrier, inc=1, device_id={"tm": t, "rows": r + 1}, device_id_type=MESH)

    @pl.when(has_below)
    def _():
        pl.semaphore_signal(barrier, inc=1, device_id={"tm": t, "rows": r - 1}, device_id_type=MESH)

    for field in (act, mid):

        @pl.when(t == 0)
        def _(field=field):
            field[0:2] = jnp.zeros((2,) + field.shape[1:], BF16)

        @pl.when(r == 0)
        def _(field=field):
            for frame in range(4):
                field[frame, 0] = jnp.zeros((COLS, chans), BF16)

        @pl.when(r == blocks - 1)
        def _(field=field):
            for frame in range(4):
                field[frame, 5] = jnp.zeros((COLS, chans), BF16)

    loads[0].wait()
    loads[1].wait()
    gain = norm_gain[...].astype(F32)
    for frame in range(2):
        for row in range(4):
            wide = video[frame, row].astype(F32)
            act[frame + 2, row + 1] = padded(silu(rms_norm(wide, gain))).astype(BF16)

    pl.semaphore_wait(
        barrier, steps - 1 + has_above.astype(jnp.int32) + has_below.astype(jnp.int32)
    )

    def halo(which, field, slot, src, dst, device):
        return pltpu.make_async_remote_copy(
            src_ref=field.at[src],
            dst_ref=field.at[dst],
            send_sem=halo_send.at[which, slot],
            recv_sem=halo_recv.at[which, slot],
            device_id=device,
            device_id_type=MESH,
        )

    own, past = (pl.ds(2, 2), pl.ds(0, 2))

    def copies(which, field):
        later = {"tm": jnp.minimum(t + 1, steps - 1), "rows": r}
        above = {"tm": t, "rows": jnp.minimum(r + 1, blocks - 1)}
        below = {"tm": t, "rows": jnp.maximum(r - 1, 0)}
        return {
            "inner": halo(which, field, 0, (own, pl.ds(2, 2)), (past, pl.ds(2, 2)), later),
            "low": halo(which, field, 1, (own, 1), (past, 1), later),
            "high": halo(which, field, 2, (own, 4), (past, 4), later),
            "up": halo(which, field, 3, (own, 4), (own, 0), above),
            "down": halo(which, field, 4, (own, 1), (own, 5), below),
            "on_low": halo(which, field, 5, (own, 0), (past, 0), later),
            "on_high": halo(which, field, 6, (own, 5), (past, 5), later),
        }

    def when(flag, action):
        pl.when(flag)(action)

    def local_part(field, weight):
        for frame in range(2):
            early = range(2 - frame, 3)
            for rows, span in (((1, 2), (0, 1, 2)), ((0,), (1, 2)), ((3,), (0, 1))):
                pairs = [(a, b) for a in early for b in span]
                total = jnp.dot(
                    cells_of(field, frame, pairs, rows),
                    taps_of(weight, pairs),
                    preferred_element_type=F32,
                )
                for i, row in enumerate(rows):
                    acc[frame, row] = total[i * COLS : (i + 1) * COLS]

    def past_part(field, weight, parts, finish):
        for frame in range(2):
            early = range(0, 2 - frame)
            for rows, span in parts:
                pairs = [(a, b) for a in early for b in span]
                total = jnp.dot(
                    cells_of(field, frame, pairs, rows),
                    taps_of(weight, pairs),
                    preferred_element_type=F32,
                )
                for i, row in enumerate(rows):
                    part = acc[frame, row] + total[i * COLS : (i + 1) * COLS]
                    if finish is None:
                        acc[frame, row] = part
                    else:
                        finish(frame, row, part)

    def edge_part(field, weight, finish):
        for frame in range(2):
            for row, b in ((0, 0), (3, 2)):
                pairs = [(a, b) for a in range(3)]
                total = jnp.dot(
                    cells_of(field, frame, pairs, (row,)),
                    taps_of(weight, pairs),
                    preferred_element_type=F32,
                )
                finish(frame, row, acc[frame, row] + total)

    inner_rows = (((1, 2), (0, 1, 2)),)
    outer_rows = (((0,), (1, 2)), ((3,), (0, 1)))

    def to_mid(frame, row, total):
        mid[frame + 2, row + 1] = padded(silu(column_sum(total))).astype(BF16)

    def to_hidden(frame, row, total):
        acc[frame, row, :, 0:chans] = padded(
            video[frame, row].astype(F32) + column_sum(total)
        )

    def pack_hidden(rows):
        for row in rows:
            one, two = (
                acc[frame, row, :, 0:chans].reshape(PER_ROW, UNIT, chans) for frame in range(2)
            )
            hidden[row] = jnp.concatenate([one, two], axis=1).astype(BF16)

    chunk_rows = ((1, 2), (0, 3))

    def unit_of(chunk, peer):
        half = peer // PER_ROW
        first_row, second_row = chunk_rows[chunk]
        return (first_row + half * (second_row - first_row), lax.rem(peer, PER_ROW))

    def forth(chunk, peer):
        row, place = unit_of(chunk, peer)
        return pltpu.make_async_remote_copy(
            src_ref=hidden.at[row, place],
            dst_ref=gathered.at[chunk, t],
            send_sem=swap_send.at[0, chunk],
            recv_sem=swap_recv.at[0, chunk],
            device_id={"tm": peer, "rows": r},
            device_id_type=MESH,
        )

    def back(chunk, peer):
        return pltpu.make_async_remote_copy(
            src_ref=answer.at[chunk, peer],
            dst_ref=returned.at[chunk, t],
            send_sem=swap_send.at[1, chunk],
            recv_sem=swap_recv.at[1, chunk],
            device_id={"tm": peer, "rows": r},
            device_id_type=MESH,
        )

    def send_all(make, chunk):
        def body(j, _):
            make(chunk, lax.rem(t + j, steps)).start()
            return 0

        lax.fori_loop(1, steps, body, 0)

    def scatter(chunk):
        send_all(forth, chunk)
        row, place = unit_of(chunk, t)
        pltpu.make_async_copy(
            hidden.at[row, place], gathered.at[chunk, t], swap_recv.at[0, chunk]
        ).start()

    def attend(chunk):
        pltpu.make_async_copy(
            gathered.at[chunk], gathered.at[chunk], swap_recv.at[0, chunk]
        ).wait()
        cells = steps * 2 * UNIT
        wide = gathered[chunk].reshape(cells, chans).astype(F32)
        normed = rms_norm(wide, attn_gain[...].astype(F32)).astype(BF16)
        joined = jnp.concatenate([query_w[...], key_w[...], value_w[...]], axis=1)
        projected = jnp.dot(normed, joined, preferred_element_type=F32).astype(BF16)
        query = projected[:, :chans]
        key = projected[:, chans : 2 * chans]
        value = projected[:, 2 * chans :]
        tile = 128
        spot = lax.broadcasted_iota(jnp.int32, (tile, tile), 0)
        other = lax.broadcasted_iota(jnp.int32, (tile, tile), 1)
        same = lax.rem(spot, UNIT) == lax.rem(other, UNIT)
        causal = same & (other <= spot)
        root = 1.0 / jnp.sqrt(F32(chans))
        for i in range(cells // tile):
            rows = slice(i * tile, (i + 1) * tile)
            scores = lax.dot_general(
                query[rows],
                key[: (i + 1) * tile],
                (((1,), (1,)), ((), ())),
                preferred_element_type=F32,
            ) * root
            tiles = [
                jnp.where(
                    causal if j == i else same, scores[:, j * tile : (j + 1) * tile], F32(-1e30)
                )
                for j in range(i + 1)
            ]
            top = jnp.max(functools.reduce(jnp.maximum, tiles), axis=1, keepdims=True)
            weights = [jnp.exp(part - top) for part in tiles]
            total = jnp.sum(functools.reduce(jnp.add, weights), axis=1, keepdims=True)
            mixed = jnp.dot(
                jnp.concatenate([part.astype(BF16) for part in weights], axis=1),
                value[: (i + 1) * tile],
                preferred_element_type=F32,
            )
            mixed = (mixed / total).astype(BF16)
            shown = wide[rows] + jnp.dot(mixed, out_w[...], preferred_element_type=F32)
            count = tile // (2 * UNIT)
            answer[chunk, i * count : (i + 1) * count] = (
                shown.astype(BF16).reshape(count, 2 * UNIT, chans)
            )
        send_all(back, chunk)
        pltpu.make_async_copy(
            answer.at[chunk, t], returned.at[chunk, t], swap_recv.at[1, chunk]
        ).start()

    def collect(chunk):
        pltpu.make_async_copy(
            returned.at[chunk], returned.at[chunk], swap_recv.at[1, chunk]
        ).wait()
        for half, row in enumerate(chunk_rows[chunk]):
            units = returned[chunk, half * PER_ROW : (half + 1) * PER_ROW].astype(F32)
            for frame in range(2):
                part = units[:, frame * UNIT : (frame + 1) * UNIT].reshape(COLS, chans)
                result_ref[frame, row] = part[: COLS - UNIT].astype(BF16)

    one = copies(0, act)
    when(has_above, one["up"].start)
    when(has_below, one["down"].start)
    for name in ("inner", "low", "high"):
        when(has_next, one[name].start)
    loads[2].wait()
    local_part(act, first)
    for name in ("inner", "low", "high"):
        when(has_prev, one[name].wait_recv)
    two = copies(1, mid)
    past_part(act, first, inner_rows, to_mid)
    when(has_next, two["inner"].start)
    past_part(act, first, outer_rows, None)

    def pass_on(copy):
        when(has_below, copy["up"].wait_recv)
        when(has_below & has_next, copy["on_low"].start)
        when(has_above, copy["down"].wait_recv)
        when(has_above & has_next, copy["on_high"].start)

    def passed_on(copy):
        when(has_below & has_prev, copy["on_low"].wait_recv)
        when(has_above & has_prev, copy["on_high"].wait_recv)

    pass_on(one)
    passed_on(one)
    edge_part(act, first, to_mid)

    when(has_above, two["up"].start)
    when(has_below, two["down"].start)
    for name in ("low", "high"):
        when(has_next, two[name].start)
    loads[3].wait()
    local_part(mid, second)
    for name in ("inner", "low", "high"):
        when(has_prev, two[name].wait_recv)
    past_part(mid, second, inner_rows, to_hidden)
    pack_hidden((1, 2))
    scatter(0)
    past_part(mid, second, outer_rows, None)
    pass_on(two)
    passed_on(two)
    edge_part(mid, second, to_hidden)
    pack_hidden((0, 3))
    scatter(1)

    for load in loads[4:]:
        load.wait()
    attend(0)
    attend(1)
    collect(0)
    collect(1)

    for copy in (one, two):
        when(has_above, copy["up"].wait_send)
        when(has_below, copy["down"].wait_send)
        for name in ("inner", "low", "high"):
            when(has_next, copy[name].wait_send)
        when(has_below & has_next, copy["on_low"].wait_send)
        when(has_above & has_next, copy["on_high"].wait_send)
    for way in range(2):
        for chunk in range(2):
            sent = gathered.at[chunk, pl.ds(0, steps - 1)]
            pltpu.make_async_copy(sent, sent, swap_send.at[way, chunk]).wait()


def local(video, norm_gain, first, second, attn_gain, query_w, key_w, value_w, out_w):
    steps, blocks = (lax.axis_size("tm"), lax.axis_size("rows"))
    frames, height, width, chans = video.shape
    anywhere = pl.BlockSpec(memory_space=pl.ANY)
    square = (chans, chans)
    return pl.pallas_call(
        functools.partial(kernel, steps, blocks),
        out_shape=jax.ShapeDtypeStruct(video.shape, video.dtype),
        in_specs=[anywhere] * 9,
        out_specs=pl.BlockSpec(memory_space=pltpu.VMEM),
        scratch_shapes=[
            pltpu.VMEM(video.shape, BF16),
            pltpu.VMEM((1, chans), BF16),
            pltpu.VMEM((3, 3, 3) + square, BF16),
            pltpu.VMEM((3, 3, 3) + square, BF16),
            pltpu.VMEM((1, chans), BF16),
            pltpu.VMEM(square, BF16),
            pltpu.VMEM(square, BF16),
            pltpu.VMEM(square, BF16),
            pltpu.VMEM(square, BF16),
            pltpu.VMEM((4, 6, COLS, chans), BF16),
            pltpu.VMEM((4, 6, COLS, chans), BF16),
            pltpu.VMEM((2, 4, COLS, 3 * chans), F32),
            pltpu.VMEM((4, PER_ROW, 2 * UNIT, chans), BF16),
            pltpu.VMEM((2, steps, 2 * UNIT, chans), BF16),
            pltpu.VMEM((2, steps, 2 * UNIT, chans), BF16),
            pltpu.VMEM((2, steps, 2 * UNIT, chans), BF16),
            pltpu.SemaphoreType.DMA((9,)),
            pltpu.SemaphoreType.DMA((2, 7)),
            pltpu.SemaphoreType.DMA((2, 7)),
            pltpu.SemaphoreType.DMA((2, 2)),
            pltpu.SemaphoreType.DMA((2, 2)),
        ],
        compiler_params=pltpu.CompilerParams(
            collective_id=0, has_side_effects=True, vmem_limit_bytes=56 * 1024 * 1024
        ),
    )(
        video,
        norm_gain.reshape(1, chans),
        first,
        second,
        attn_gain.reshape(1, chans),
        query_w,
        key_w,
        value_w,
        out_w,
    )


def solution(mesh):
    return jax.shard_map(
        local,
        mesh=mesh,
        in_specs=(P("tm", "rows", None, None), P(), P(), P(), P(), P(), P(), P(), P()),
        out_specs=P("tm", "rows", None, None),
        check_vma=False,
    )
```

```python
import functools

import jax
import jax.numpy as jnp
from jax import lax
from jax.experimental import pallas as pl
from jax.experimental.pallas import tpu as pltpu
from jax.sharding import PartitionSpec as P

F32 = jnp.float32
BF16 = jnp.bfloat16
MESH = pl.DeviceIdType.MESH
COLS = 128
UNIT = 8
PER_ROW = COLS // UNIT


def rms_norm(wide, gain):
    scale = lax.rsqrt(jnp.mean(wide * wide, axis=-1, keepdims=True) + 1e-06)
    return wide * scale * gain


def silu(v):
    return v / (1.0 + jnp.exp(-v))


def column_sum(total):
    width, chans = (COLS - UNIT, total.shape[1] // 3)
    left = pltpu.roll(total[:, :chans], 1, 0)
    right = pltpu.roll(total[:, 2 * chans :], COLS - 1, 0)
    return (left + total[:, chans : 2 * chans] + right)[:width]


def padded(value):
    return jnp.concatenate([value, jnp.zeros((COLS - value.shape[0], value.shape[1]), F32)], axis=0)


def kernel(
    steps,
    blocks,
    video_hbm,
    norm_gain_hbm,
    first_hbm,
    second_hbm,
    attn_gain_hbm,
    query_hbm,
    key_hbm,
    value_hbm,
    out_hbm,
    result_ref,
    video,
    norm_gain,
    first,
    second,
    attn_gain,
    query_w,
    key_w,
    value_w,
    out_w,
    act,
    mid,
    acc,
    hidden,
    gathered,
    answer,
    returned,
    load_sem,
    halo_send,
    halo_recv,
    swap_send,
    swap_recv,
):
    t, r = (lax.axis_index("tm"), lax.axis_index("rows"))
    chans = video.shape[-1]
    loads = [
        pltpu.make_async_copy(src, dst, load_sem.at[i])
        for i, (src, dst) in enumerate(
            [
                (video_hbm, video),
                (norm_gain_hbm, norm_gain),
                (first_hbm, first),
                (second_hbm, second),
                (attn_gain_hbm, attn_gain),
                (query_hbm, query_w),
                (key_hbm, key_w),
                (value_hbm, value_w),
                (out_hbm, out_w),
            ]
        )
    ]
    for load in loads:
        load.start()

    has_next, has_prev = (t < steps - 1, t > 0)
    has_above, has_below = (r < blocks - 1, r > 0)

    barrier = pltpu.get_barrier_semaphore()

    def greet(j, _):
        peer = lax.rem(t + j, steps)
        pl.semaphore_signal(barrier, inc=1, device_id={"tm": peer, "rows": r}, device_id_type=MESH)
        return 0

    lax.fori_loop(1, steps, greet, 0)

    @pl.when(has_above)
    def _():
        pl.semaphore_signal(barrier, inc=1, device_id={"tm": t, "rows": r + 1}, device_id_type=MESH)

    @pl.when(has_below)
    def _():
        pl.semaphore_signal(barrier, inc=1, device_id={"tm": t, "rows": r - 1}, device_id_type=MESH)

    flip = (lax.rem(r, 4) < 2).astype(jnp.int32)

    def place(q):
        return q + flip * (3 - 2 * q)

    def line(q):
        return q + 1 + flip * (3 - 2 * q)

    def tap(b):
        return b + flip * (2 - 2 * b)

    for field in (act, mid):

        @pl.when(t == 0)
        def _(field=field):
            field[0:2] = jnp.zeros((2,) + field.shape[1:], BF16)

        @pl.when(r == 0)
        def _(field=field):
            for frame in range(4):
                field[frame, 0] = jnp.zeros((COLS, chans), BF16)

        @pl.when(r == blocks - 1)
        def _(field=field):
            for frame in range(4):
                field[frame, 5] = jnp.zeros((COLS, chans), BF16)

    loads[0].wait()
    loads[1].wait()
    gain = norm_gain[...].astype(F32)
    for frame in range(2):
        for row in range(4):
            wide = video[frame, row].astype(F32)
            act[frame + 2, row + 1] = padded(silu(rms_norm(wide, gain))).astype(BF16)

    pl.semaphore_wait(
        barrier, steps - 1 + has_above.astype(jnp.int32) + has_below.astype(jnp.int32)
    )

    def halo(which, field, slot, src, dst, device):
        return pltpu.make_async_remote_copy(
            src_ref=field.at[src],
            dst_ref=field.at[dst],
            send_sem=halo_send.at[which, slot],
            recv_sem=halo_recv.at[which, slot],
            device_id=device,
            device_id_type=MESH,
        )

    own, past = (pl.ds(2, 2), pl.ds(0, 2))
    has_near = jnp.where(flip == 1, has_above, has_below)
    has_far = jnp.where(flip == 1, has_below, has_above)

    def copies(which, field):
        later = {"tm": jnp.minimum(t + 1, steps - 1), "rows": r}
        near = {"tm": t, "rows": jnp.clip(r - 1 + 2 * flip, 0, blocks - 1)}
        far = {"tm": t, "rows": jnp.clip(r + 1 - 2 * flip, 0, blocks - 1)}
        onward, backward = (5 * flip, 5 - 5 * flip)
        return {
            "inner": halo(which, field, 0, (own, pl.ds(2, 2)), (past, pl.ds(2, 2)), later),
            "first": halo(which, field, 1, (own, line(0)), (past, line(0)), later),
            "last": halo(which, field, 2, (own, line(3)), (past, line(3)), later),
            "to_near": halo(which, field, 4 - flip, (own, line(0)), (own, backward), near),
            "to_far": halo(which, field, 3 + flip, (own, line(3)), (own, onward), far),
            "from_near": halo(which, field, 3 + flip, (own, line(0)), (own, onward), near),
            "from_far": halo(which, field, 4 - flip, (own, line(3)), (own, backward), far),
            "on_near": halo(which, field, 5, (own, onward), (past, onward), later),
            "on_far": halo(which, field, 6, (own, backward), (past, backward), later),
        }

    def when(flag, action):
        pl.when(flag)(action)

    def product(field, weight, frame, early, rows, span):
        pairs = [(a, b) for a in early for b in span]
        cells = jnp.concatenate(
            [
                jnp.concatenate([field[frame + a, line(q + b - 1)] for q in rows], axis=0)
                for a, b in pairs
            ],
            axis=1,
        )
        taps = jnp.concatenate(
            [
                jnp.concatenate([weight[a, tap(b), e] for e in range(3)], axis=1)
                for a, b in pairs
            ],
            axis=0,
        )
        return jnp.dot(cells, taps, preferred_element_type=F32)

    def part(total, i):
        return total[i * COLS : (i + 1) * COLS]

    every = (0, 1, 2)
    groups = (((1, 2), every), ((0,), (1, 2)), ((3,), (0, 1)))

    def to_mid(frame, q, total):
        mid[frame + 2, line(q)] = padded(silu(column_sum(total))).astype(BF16)

    def to_hidden(q, totals):
        one, two = (
            padded(video[frame, place(q)].astype(F32) + column_sum(total)).reshape(
                PER_ROW, UNIT, chans
            )
            for frame, total in enumerate(totals)
        )
        hidden[q] = jnp.concatenate([one, two], axis=1).astype(BF16)

    parity = lax.rem(t, 2)

    def peer_copy(src, dst, send, recv, peer):
        return pltpu.make_async_remote_copy(
            src_ref=src,
            dst_ref=dst,
            send_sem=send,
            recv_sem=recv,
            device_id={"tm": peer, "rows": r},
            device_id_type=MESH,
        )

    def scatter_all():
        def body(j, _):
            peer = lax.rem(t + j, steps)
            peer_copy(
                hidden.at[peer // PER_ROW, lax.rem(peer, PER_ROW)],
                gathered.at[0, t],
                swap_send.at[0, 0],
                swap_recv.at[0, 0],
                peer,
            ).start()
            return 0

        lax.fori_loop(1, steps, body, 0)
        pltpu.make_async_copy(
            hidden.at[t // PER_ROW, lax.rem(t, PER_ROW)], gathered.at[0, t], swap_recv.at[0, 0]
        ).start()

    def scatter_half(odd):
        def send(j):
            spot = lax.rem(t // 2 + j, PER_ROW)
            peer_copy(
                hidden.at[2 + odd, spot],
                gathered.at[1, t],
                swap_send.at[0, 1 + odd],
                swap_recv.at[0, 1],
                2 * spot + odd,
            ).start()

        def body(j, _):
            send(j)
            return 0

        lax.fori_loop(1, PER_ROW, body, 0)
        pl.when(parity != odd)(lambda: send(0))
        pl.when(parity == odd)(
            pltpu.make_async_copy(
                hidden.at[2 + odd, t // 2], gathered.at[1, t], swap_recv.at[0, 1]
            ).start
        )

    def attend(slot):
        pltpu.make_async_copy(gathered.at[slot], gathered.at[slot], swap_recv.at[0, slot]).wait()
        cells = steps * 2 * UNIT
        wide = gathered[slot].reshape(cells, chans).astype(F32)
        normed = rms_norm(wide, attn_gain[...].astype(F32)).astype(BF16)
        joined = jnp.concatenate([query_w[...], key_w[...], value_w[...]], axis=1)
        projected = jnp.dot(normed, joined, preferred_element_type=F32).astype(BF16)
        query = projected[:, :chans]
        key = projected[:, chans : 2 * chans]
        value = projected[:, 2 * chans :]
        tile = 128
        spot = lax.broadcasted_iota(jnp.int32, (tile, tile), 0)
        other = lax.broadcasted_iota(jnp.int32, (tile, tile), 1)
        same = lax.rem(spot, UNIT) == lax.rem(other, UNIT)
        causal = same & (other <= spot)
        root = 1.0 / jnp.sqrt(F32(chans))
        for i in range(cells // tile):
            rows = slice(i * tile, (i + 1) * tile)
            scores = (
                lax.dot_general(
                    query[rows],
                    key[: (i + 1) * tile],
                    (((1,), (1,)), ((), ())),
                    preferred_element_type=F32,
                )
                * root
            )
            tiles = [
                jnp.where(
                    causal if j == i else same, scores[:, j * tile : (j + 1) * tile], F32(-1e30)
                )
                for j in range(i + 1)
            ]
            top = jnp.max(functools.reduce(jnp.maximum, tiles), axis=1, keepdims=True)
            weights = [jnp.exp(one - top) for one in tiles]
            total = jnp.sum(functools.reduce(jnp.add, weights), axis=1, keepdims=True)
            mixed = jnp.dot(
                jnp.concatenate([one.astype(BF16) for one in weights], axis=1),
                value[: (i + 1) * tile],
                preferred_element_type=F32,
            )
            mixed = (mixed / total).astype(BF16)
            shown = wide[rows] + jnp.dot(mixed, out_w[...], preferred_element_type=F32)
            count = tile // (2 * UNIT)
            answer[slot, i * count : (i + 1) * count] = shown.astype(BF16).reshape(
                count, 2 * UNIT, chans
            )
        if slot == 0:
            home = returned.at[t // PER_ROW, lax.rem(t, PER_ROW)]
            arrived = swap_recv.at[1, 0]
        else:
            home = returned.at[2 + parity, t // 2]
            arrived = swap_recv.at[1, 1 + parity]

        def body(j, _):
            peer = lax.rem(t + j, steps)
            peer_copy(answer.at[slot, peer], home, swap_send.at[1, slot], arrived, peer).start()
            return 0

        lax.fori_loop(1, steps, body, 0)
        pltpu.make_async_copy(answer.at[slot, t], home, arrived).start()

    def collect(index, rows):
        block = returned.at[pl.ds(rows[0], len(rows))]
        pltpu.make_async_copy(block, block, swap_recv.at[1, index]).wait()
        for q in rows:
            units = returned[q].astype(F32)
            for frame in range(2):
                cols = units[:, frame * UNIT : (frame + 1) * UNIT].reshape(COLS, chans)
                result_ref[frame, place(q)] = cols[: COLS - UNIT].astype(BF16)

    one, two = (copies(0, act), copies(1, mid))
    when(has_far, one["to_far"].start)
    when(has_near, one["to_near"].start)
    for name in ("inner", "first", "last"):
        when(has_next, one[name].start)
    loads[2].wait()
    for frame in range(2):
        for rows, span in groups:
            total = product(act, first, frame, range(2 - frame, 3), rows, span)
            for i, q in enumerate(rows):
                acc[frame, q] = part(total, i)
    for name in ("inner", "first", "last"):
        when(has_prev, one[name].wait_recv)
    for rows, span in groups:
        for frame in range(2):
            total = product(act, first, frame, range(0, 2 - frame), rows, span)
            for i, q in enumerate(rows):
                if len(rows) == 2:
                    to_mid(frame, q, acc[frame, q] + part(total, i))
                else:
                    acc[frame, q] += part(total, i)
        if len(rows) == 2:
            when(has_next, two["inner"].start)

    def edge(field, weight, q):
        return [
            acc[frame, q] + product(field, weight, frame, every, (q,), (0,) if q == 0 else (2,))
            for frame in range(2)
        ]

    def take(copy, side, present):
        when(present, copy["from_" + side].wait_recv)
        when(present & has_next, copy["on_" + side].start)

    def taken(copy, side, present):
        when(present & has_prev, copy["on_" + side].wait_recv)

    take(one, "near", has_near)
    taken(one, "near", has_near)
    for frame, total in enumerate(edge(act, first, 0)):
        to_mid(frame, 0, total)
    when(has_near, two["to_near"].start)
    when(has_next, two["first"].start)
    take(one, "far", has_far)
    taken(one, "far", has_far)
    for frame, total in enumerate(edge(act, first, 3)):
        to_mid(frame, 3, total)
    when(has_far, two["to_far"].start)
    when(has_next, two["last"].start)

    loads[3].wait()
    for name in ("inner", "first"):
        when(has_prev, two[name].wait_recv)
    to_hidden(1, [product(mid, second, frame, every, (1,), every) for frame in range(2)])
    for frame in range(2):
        acc[frame, 0] = product(mid, second, frame, every, (0,), (1, 2))
    take(two, "near", has_near)
    when(has_prev, two["last"].wait_recv)
    to_hidden(2, [product(mid, second, frame, every, (2,), every) for frame in range(2)])
    taken(two, "near", has_near)
    to_hidden(0, edge(mid, second, 0))
    scatter_all()
    scatter_half(0)
    for frame in range(2):
        acc[frame, 3] = product(mid, second, frame, every, (3,), (0, 1))
    take(two, "far", has_far)
    taken(two, "far", has_far)
    to_hidden(3, edge(mid, second, 3))
    scatter_half(1)

    for load in loads[4:]:
        load.wait()
    attend(0)
    attend(1)
    collect(0, (0, 1))
    collect(1, (2,))
    collect(2, (3,))

    for copy in (one, two):
        for side, present in (("near", has_near), ("far", has_far)):
            when(present, copy["to_" + side].wait_send)
            when(present & has_next, copy["on_" + side].wait_send)
        for name in ("inner", "first", "last"):
            when(has_next, copy[name].wait_send)

    def gone(count, sem):
        sent = gathered.at[0, pl.ds(0, count)]
        pltpu.make_async_copy(sent, sent, sem).wait()

    gone(steps - 1, swap_send.at[0, 0])
    for odd in range(2):
        pl.when(parity == odd)(lambda odd=odd: gone(PER_ROW - 1, swap_send.at[0, 1 + odd]))
        pl.when(parity != odd)(lambda odd=odd: gone(PER_ROW, swap_send.at[0, 1 + odd]))
    for slot in range(2):
        gone(steps - 1, swap_send.at[1, slot])


def local(video, norm_gain, first, second, attn_gain, query_w, key_w, value_w, out_w):
    steps, blocks = (lax.axis_size("tm"), lax.axis_size("rows"))
    frames, height, width, chans = video.shape
    anywhere = pl.BlockSpec(memory_space=pl.ANY)
    square = (chans, chans)
    return pl.pallas_call(
        functools.partial(kernel, steps, blocks),
        out_shape=jax.ShapeDtypeStruct(video.shape, video.dtype),
        in_specs=[anywhere] * 9,
        out_specs=pl.BlockSpec(memory_space=pltpu.VMEM),
        scratch_shapes=[
            pltpu.VMEM(video.shape, BF16),
            pltpu.VMEM((1, chans), BF16),
            pltpu.VMEM((3, 3, 3) + square, BF16),
            pltpu.VMEM((3, 3, 3) + square, BF16),
            pltpu.VMEM((1, chans), BF16),
            pltpu.VMEM(square, BF16),
            pltpu.VMEM(square, BF16),
            pltpu.VMEM(square, BF16),
            pltpu.VMEM(square, BF16),
            pltpu.VMEM((4, 6, COLS, chans), BF16),
            pltpu.VMEM((4, 6, COLS, chans), BF16),
            pltpu.VMEM((2, 4, COLS, 3 * chans), F32),
            pltpu.VMEM((4, PER_ROW, 2 * UNIT, chans), BF16),
            pltpu.VMEM((2, steps, 2 * UNIT, chans), BF16),
            pltpu.VMEM((2, steps, 2 * UNIT, chans), BF16),
            pltpu.VMEM((4, PER_ROW, 2 * UNIT, chans), BF16),
            pltpu.SemaphoreType.DMA((9,)),
            pltpu.SemaphoreType.DMA((2, 7)),
            pltpu.SemaphoreType.DMA((2, 7)),
            pltpu.SemaphoreType.DMA((2, 3)),
            pltpu.SemaphoreType.DMA((2, 3)),
        ],
        compiler_params=pltpu.CompilerParams(
            collective_id=0, has_side_effects=True, vmem_limit_bytes=56 * 1024 * 1024
        ),
    )(
        video,
        norm_gain.reshape(1, chans),
        first,
        second,
        attn_gain.reshape(1, chans),
        query_w,
        key_w,
        value_w,
        out_w,
    )


def solution(mesh):
    return jax.shard_map(
        local,
        mesh=mesh,
        in_specs=(P("tm", "rows", None, None), P(), P(), P(), P(), P(), P(), P(), P()),
        out_specs=P("tm", "rows", None, None),
        check_vma=False,
    )
```

```python
import functools

import jax
import jax.numpy as jnp
from jax import lax
from jax.experimental import pallas as pl
from jax.experimental.pallas import tpu as pltpu
from jax.sharding import PartitionSpec as P

F32 = jnp.float32
BF16 = jnp.bfloat16
MESH = pl.DeviceIdType.MESH
COLS = 128
UNIT = 8
PER_ROW = COLS // UNIT


def rms_norm(wide, gain):
    scale = lax.rsqrt(jnp.mean(wide * wide, axis=-1, keepdims=True) + 1e-06)
    return wide * scale * gain


def silu(v):
    return v / (1.0 + jnp.exp(-v))


def column_sum(total):
    width, chans = (COLS - UNIT, total.shape[1] // 3)
    left = pltpu.roll(total[:, :chans], 1, 0)
    right = pltpu.roll(total[:, 2 * chans :], COLS - 1, 0)
    return (left + total[:, chans : 2 * chans] + right)[:width]


def padded(value):
    return jnp.concatenate([value, jnp.zeros((COLS - value.shape[0], value.shape[1]), F32)], axis=0)


def kernel(
    steps,
    blocks,
    video_hbm,
    norm_gain_hbm,
    first_hbm,
    second_hbm,
    attn_gain_hbm,
    query_hbm,
    key_hbm,
    value_hbm,
    out_hbm,
    result_ref,
    video,
    norm_gain,
    first,
    second,
    attn_gain,
    query_w,
    key_w,
    value_w,
    out_w,
    act,
    mid,
    acc,
    hidden,
    gathered,
    answer,
    returned,
    load_sem,
    halo_send,
    halo_recv,
    swap_send,
    swap_recv,
):
    t, r = (lax.axis_index("tm"), lax.axis_index("rows"))
    chans = video.shape[-1]
    loads = [
        pltpu.make_async_copy(src, dst, load_sem.at[i])
        for i, (src, dst) in enumerate(
            [
                (video_hbm, video),
                (norm_gain_hbm, norm_gain),
                (first_hbm, first),
                (second_hbm, second),
                (attn_gain_hbm, attn_gain),
                (query_hbm, query_w),
                (key_hbm, key_w),
                (value_hbm, value_w),
                (out_hbm, out_w),
            ]
        )
    ]
    for load in loads:
        load.start()

    has_next, has_prev = (t < steps - 1, t > 0)
    has_above, has_below = (r < blocks - 1, r > 0)

    barrier = pltpu.get_barrier_semaphore()

    def greet(j, _):
        peer = lax.rem(t + j, steps)
        pl.semaphore_signal(barrier, inc=1, device_id={"tm": peer, "rows": r}, device_id_type=MESH)
        return 0

    lax.fori_loop(1, steps, greet, 0)

    met = steps - 1
    for side, there in ((1, has_above), (-1, has_below)):
        for shift, then in ((0, True), (1, has_next), (-1, has_prev)):
            present = there if shift == 0 else there & then
            peer = {"tm": t + shift, "rows": r + side}
            met = met + present.astype(jnp.int32)

            @pl.when(present)
            def _(peer=peer):
                pl.semaphore_signal(barrier, inc=1, device_id=peer, device_id_type=MESH)

    flip = (lax.rem(r, 4) < 2).astype(jnp.int32)

    def place(q):
        return q + flip * (3 - 2 * q)

    def line(q):
        return q + 2 + flip * (3 - 2 * q)

    def tap(b):
        return b + flip * (2 - 2 * b)

    for field in (act, mid):

        @pl.when(t == 0)
        def _(field=field):
            field[0:2] = jnp.zeros((2,) + field.shape[1:], BF16)

        @pl.when(r == 0)
        def _(field=field):
            for frame in range(4):
                field[frame, 1] = jnp.zeros((COLS, chans), BF16)

        @pl.when(r == blocks - 1)
        def _(field=field):
            for frame in range(4):
                field[frame, 6] = jnp.zeros((COLS, chans), BF16)

    loads[0].wait()
    loads[1].wait()
    gain = norm_gain[...].astype(F32)
    for frame in range(2):
        for row in range(4):
            wide = video[frame, row].astype(F32)
            act[frame + 2, row + 2] = padded(silu(rms_norm(wide, gain))).astype(BF16)

    pl.semaphore_wait(barrier, met)

    def halo(which, field, slots, src, dst, device):
        return pltpu.make_async_remote_copy(
            src_ref=field.at[src],
            dst_ref=field.at[dst],
            send_sem=halo_send.at[which, slots[0]],
            recv_sem=halo_recv.at[which, slots[1]],
            device_id=device,
            device_id_type=MESH,
        )

    own, past = (pl.ds(2, 2), pl.ds(0, 2))
    has_far = jnp.where(flip == 1, has_below, has_above)
    slow = has_far & ((lax.rem(r, 4) == 0) | (lax.rem(r, 4) == 3))
    fast = has_far & ~((lax.rem(r, 4) == 0) | (lax.rem(r, 4) == 3))

    def copies(which, field):
        next_t = jnp.minimum(t + 1, steps - 1)
        near_r = jnp.clip(r - 1 + 2 * flip, 0, blocks - 1)
        far_r = jnp.clip(r + 1 - 2 * flip, 0, blocks - 1)
        later, near, far, next_near, next_far = (
            {"tm": a, "rows": b}
            for a, b in ((next_t, r), (t, near_r), (t, far_r), (next_t, near_r), (next_t, far_r))
        )
        near_land, far_land = (6 - 5 * flip, 1 + 5 * flip)
        far_in, far_in2 = (line(4), line(5))
        inner = pl.ds(3, 2)
        return {
            "inner": halo(which, field, (0, 0), (own, inner), (past, inner), later),
            "first": halo(which, field, (1, 1), (own, line(0)), (past, line(0)), later),
            "last": halo(which, field, (2, 2), (own, line(3)), (past, line(3)), later),
            "to_near": halo(which, field, (3, 4 - flip), (own, line(0)), (own, near_land), near),
            "to_far": halo(which, field, (4, 3 + flip), (own, line(3)), (own, far_land), far),
            "diag_near": halo(
                which, field, (5, 6 - flip), (own, line(0)), (past, near_land), next_near
            ),
            "diag_far": halo(
                which, field, (6, 5 + flip), (own, line(3)), (past, far_land), next_far
            ),
            "from_near": halo(which, field, (3, 3 + flip), (own, line(0)), (own, line(-1)), near),
            "from_far": halo(which, field, (4, 4 - flip), (own, line(3)), (own, far_in), far),
            "past_near": halo(which, field, (5, 5 + flip), (own, line(0)), (past, line(-1)), later),
            "on_far": halo(which, field, (7, 6 - flip), (own, far_in), (past, far_in), later),
            "to_far2": halo(which, field, (8, 7), (own, line(2)), (own, 7 * flip), far),
            "from_far2": halo(which, field, (8, 7), (own, line(2)), (own, far_in2), far),
            "on_far2": halo(which, field, (9, 8), (own, far_in2), (past, far_in2), later),
            "beyond": halo(which, field, (9, 8), (own, far_in), (past, far_in), later),
        }

    def when(flag, action):
        pl.when(flag)(action)

    def product(field, weight, frame, early, rows, span):
        pairs = [(a, b) for a in early for b in span]
        cells = jnp.concatenate(
            [
                jnp.concatenate([field[frame + a, line(q + b - 1)] for q in rows], axis=0)
                for a, b in pairs
            ],
            axis=1,
        )
        taps = jnp.concatenate(
            [
                jnp.concatenate([weight[a, tap(b), e] for e in range(3)], axis=1)
                for a, b in pairs
            ],
            axis=0,
        )
        return jnp.dot(cells, taps, preferred_element_type=F32)

    def part(total, i):
        return total[i * COLS : (i + 1) * COLS]

    every = (0, 1, 2)
    groups = (((1, 2), every), ((0,), (1, 2)), ((3,), (0, 1)))

    def to_mid(frame, q, total):
        mid[frame + 2, line(q)] = padded(silu(column_sum(total))).astype(BF16)

    def to_hidden(q, totals):
        one, two = (
            padded(video[frame, place(q)].astype(F32) + column_sum(total)).reshape(
                PER_ROW, UNIT, chans
            )
            for frame, total in enumerate(totals)
        )
        hidden[q] = jnp.concatenate([one, two], axis=1).astype(BF16)

    parity = lax.rem(t, 2)

    def peer_copy(src, dst, send, recv, peer):
        return pltpu.make_async_remote_copy(
            src_ref=src,
            dst_ref=dst,
            send_sem=send,
            recv_sem=recv,
            device_id={"tm": peer, "rows": r},
            device_id_type=MESH,
        )

    def scatter_all():
        def body(j, _):
            peer = lax.rem(t + j, steps)
            peer_copy(
                hidden.at[peer // PER_ROW, lax.rem(peer, PER_ROW)],
                gathered.at[0, t],
                swap_send.at[0, 0],
                swap_recv.at[0, 0],
                peer,
            ).start()
            return 0

        lax.fori_loop(1, steps, body, 0)
        pltpu.make_async_copy(
            hidden.at[t // PER_ROW, lax.rem(t, PER_ROW)], gathered.at[0, t], swap_recv.at[0, 0]
        ).start()

    def scatter_half(odd):
        def send(j):
            spot = lax.rem(t // 2 + j, PER_ROW)
            peer_copy(
                hidden.at[2 + odd, spot],
                gathered.at[1, t],
                swap_send.at[0, 1 + odd],
                swap_recv.at[0, 1],
                2 * spot + odd,
            ).start()

        def body(j, _):
            send(j)
            return 0

        lax.fori_loop(1, PER_ROW, body, 0)
        pl.when(parity != odd)(lambda: send(0))
        pl.when(parity == odd)(
            pltpu.make_async_copy(
                hidden.at[2 + odd, t // 2], gathered.at[1, t], swap_recv.at[0, 1]
            ).start
        )

    def attend(slot):
        pltpu.make_async_copy(gathered.at[slot], gathered.at[slot], swap_recv.at[0, slot]).wait()
        cells = steps * 2 * UNIT
        wide = gathered[slot].reshape(cells, chans).astype(F32)
        normed = rms_norm(wide, attn_gain[...].astype(F32)).astype(BF16)
        joined = jnp.concatenate([query_w[...], key_w[...], value_w[...]], axis=1)
        projected = jnp.dot(normed, joined, preferred_element_type=F32).astype(BF16)
        query = projected[:, :chans]
        key = projected[:, chans : 2 * chans]
        value = projected[:, 2 * chans :]
        tile = 128
        spot = lax.broadcasted_iota(jnp.int32, (tile, tile), 0)
        other = lax.broadcasted_iota(jnp.int32, (tile, tile), 1)
        same = lax.rem(spot, UNIT) == lax.rem(other, UNIT)
        causal = same & (other <= spot)
        root = 1.0 / jnp.sqrt(F32(chans))
        for i in range(cells // tile):
            rows = slice(i * tile, (i + 1) * tile)
            scores = (
                lax.dot_general(
                    query[rows],
                    key[: (i + 1) * tile],
                    (((1,), (1,)), ((), ())),
                    preferred_element_type=F32,
                )
                * root
            )
            tiles = [
                jnp.where(
                    causal if j == i else same, scores[:, j * tile : (j + 1) * tile], F32(-1e30)
                )
                for j in range(i + 1)
            ]
            top = jnp.max(functools.reduce(jnp.maximum, tiles), axis=1, keepdims=True)
            weights = [jnp.exp(one - top) for one in tiles]
            total = jnp.sum(functools.reduce(jnp.add, weights), axis=1, keepdims=True)
            mixed = jnp.dot(
                jnp.concatenate([one.astype(BF16) for one in weights], axis=1),
                value[: (i + 1) * tile],
                preferred_element_type=F32,
            )
            mixed = (mixed / total).astype(BF16)
            shown = wide[rows] + jnp.dot(mixed, out_w[...], preferred_element_type=F32)
            count = tile // (2 * UNIT)
            answer[slot, i * count : (i + 1) * count] = shown.astype(BF16).reshape(
                count, 2 * UNIT, chans
            )
        if slot == 0:
            home = returned.at[t // PER_ROW, lax.rem(t, PER_ROW)]
            arrived = swap_recv.at[1, 0]
        else:
            home = returned.at[2 + parity, t // 2]
            arrived = swap_recv.at[1, 1 + parity]

        def body(j, _):
            peer = lax.rem(t + j, steps)
            peer_copy(answer.at[slot, peer], home, swap_send.at[1, slot], arrived, peer).start()
            return 0

        lax.fori_loop(1, steps, body, 0)
        pltpu.make_async_copy(answer.at[slot, t], home, arrived).start()

    def collect(index, rows):
        block = returned.at[pl.ds(rows[0], len(rows))]
        pltpu.make_async_copy(block, block, swap_recv.at[1, index]).wait()
        for q in rows:
            units = returned[q].astype(F32)
            for frame in range(2):
                cols = units[:, frame * UNIT : (frame + 1) * UNIT].reshape(COLS, chans)
                result_ref[frame, place(q)] = cols[: COLS - UNIT].astype(BF16)

    one, two = (copies(0, act), copies(1, mid))
    when(has_far, one["to_far"].start)
    one["to_near"].start()
    when(has_next, one["diag_near"].start)
    when(has_next & fast, one["diag_far"].start)
    when(slow, one["to_far2"].start)
    for name in ("inner", "first", "last"):
        when(has_next, one[name].start)
    loads[2].wait()
    for frame in range(2):
        for rows, span in groups:
            total = product(act, first, frame, range(2 - frame, 3), rows, span)
            for i, q in enumerate(rows):
                acc[frame, q] = part(total, i)
    for name in ("inner", "first", "last"):
        when(has_prev, one[name].wait_recv)
    for rows, span in groups:
        for frame in range(2):
            total = product(act, first, frame, range(0, 2 - frame), rows, span)
            for i, q in enumerate(rows):
                if len(rows) == 2:
                    to_mid(frame, q, acc[frame, q] + part(total, i))
                else:
                    acc[frame, q] += part(total, i)
        if len(rows) == 2:
            when(has_next, two["inner"].start)

    def edge(field, weight, q):
        return [
            acc[frame, q] + product(field, weight, frame, every, (q,), (0,) if q == 0 else (2,))
            for frame in range(2)
        ]

    one["from_near"].wait_recv()
    when(has_prev, one["past_near"].wait_recv)
    for frame, total in enumerate(edge(act, first, 0)):
        to_mid(frame, 0, total)
    two["to_near"].start()
    when(has_next, two["diag_near"].start)
    when(has_next, two["first"].start)
    when(has_far, one["from_far"].wait_recv)
    when(has_next & slow, one["on_far"].start)
    when(has_prev & has_far, one["on_far"].wait_recv)
    for frame, total in enumerate(edge(act, first, 3)):
        to_mid(frame, 3, total)
    when(fast, two["to_far"].start)
    when(has_next & fast, two["diag_far"].start)
    when(has_next, two["last"].start)

    loads[3].wait()
    for name in ("inner", "first"):
        when(has_prev, two[name].wait_recv)
    to_hidden(1, [product(mid, second, frame, every, (1,), every) for frame in range(2)])
    for frame in range(2):
        acc[frame, 0] = product(mid, second, frame, every, (0,), (1, 2))
    two["from_near"].wait_recv()
    when(has_prev, two["past_near"].wait_recv)
    to_hidden(0, edge(mid, second, 0))
    scatter_all()

    @pl.when(slow)
    def _():
        one["from_far2"].wait_recv()
        when(has_next, one["on_far2"].start)
        when(has_prev, one["on_far2"].wait_recv)
        for frame in range(2):
            to_mid(frame, 4, product(act, first, frame, every, (4,), every))
        when(has_next, two["beyond"].start)

    when(has_prev, two["last"].wait_recv)
    to_hidden(2, [product(mid, second, frame, every, (2,), every) for frame in range(2)])
    scatter_half(0)
    for frame in range(2):
        acc[frame, 3] = product(mid, second, frame, every, (3,), (0, 1))
    when(fast, two["from_far"].wait_recv)
    when(has_prev & fast, two["on_far"].wait_recv)
    when(has_prev & slow, two["beyond"].wait_recv)
    to_hidden(3, edge(mid, second, 3))
    scatter_half(1)

    for load in loads[4:]:
        load.wait()
    attend(0)
    attend(1)
    collect(0, (0, 1))
    collect(1, (2,))
    collect(2, (3,))

    for copy in (one, two):
        copy["to_near"].wait_send()
        for name in ("inner", "first", "last", "diag_near"):
            when(has_next, copy[name].wait_send)
        when(has_next & fast, copy["diag_far"].wait_send)
    when(has_far, one["to_far"].wait_send)
    when(fast, two["to_far"].wait_send)
    when(slow, one["to_far2"].wait_send)
    for copy in (one["on_far"], one["on_far2"], two["beyond"]):
        when(has_next & slow, copy.wait_send)

    def gone(count, sem):
        sent = gathered.at[0, pl.ds(0, count)]
        pltpu.make_async_copy(sent, sent, sem).wait()

    gone(steps - 1, swap_send.at[0, 0])
    for odd in range(2):
        pl.when(parity == odd)(lambda odd=odd: gone(PER_ROW - 1, swap_send.at[0, 1 + odd]))
        pl.when(parity != odd)(lambda odd=odd: gone(PER_ROW, swap_send.at[0, 1 + odd]))
    for slot in range(2):
        gone(steps - 1, swap_send.at[1, slot])


def local(video, norm_gain, first, second, attn_gain, query_w, key_w, value_w, out_w):
    steps, blocks = (lax.axis_size("tm"), lax.axis_size("rows"))
    frames, height, width, chans = video.shape
    anywhere = pl.BlockSpec(memory_space=pl.ANY)
    square = (chans, chans)
    return pl.pallas_call(
        functools.partial(kernel, steps, blocks),
        out_shape=jax.ShapeDtypeStruct(video.shape, video.dtype),
        in_specs=[anywhere] * 9,
        out_specs=pl.BlockSpec(memory_space=pltpu.VMEM),
        scratch_shapes=[
            pltpu.VMEM(video.shape, BF16),
            pltpu.VMEM((1, chans), BF16),
            pltpu.VMEM((3, 3, 3) + square, BF16),
            pltpu.VMEM((3, 3, 3) + square, BF16),
            pltpu.VMEM((1, chans), BF16),
            pltpu.VMEM(square, BF16),
            pltpu.VMEM(square, BF16),
            pltpu.VMEM(square, BF16),
            pltpu.VMEM(square, BF16),
            pltpu.VMEM((4, 8, COLS, chans), BF16),
            pltpu.VMEM((4, 8, COLS, chans), BF16),
            pltpu.VMEM((2, 4, COLS, 3 * chans), F32),
            pltpu.VMEM((4, PER_ROW, 2 * UNIT, chans), BF16),
            pltpu.VMEM((2, steps, 2 * UNIT, chans), BF16),
            pltpu.VMEM((2, steps, 2 * UNIT, chans), BF16),
            pltpu.VMEM((4, PER_ROW, 2 * UNIT, chans), BF16),
            pltpu.SemaphoreType.DMA((9,)),
            pltpu.SemaphoreType.DMA((2, 10)),
            pltpu.SemaphoreType.DMA((2, 10)),
            pltpu.SemaphoreType.DMA((2, 3)),
            pltpu.SemaphoreType.DMA((2, 3)),
        ],
        compiler_params=pltpu.CompilerParams(
            collective_id=0, has_side_effects=True, vmem_limit_bytes=56 * 1024 * 1024
        ),
    )(
        video,
        norm_gain.reshape(1, chans),
        first,
        second,
        attn_gain.reshape(1, chans),
        query_w,
        key_w,
        value_w,
        out_w,
    )


def solution(mesh):
    return jax.shard_map(
        local,
        mesh=mesh,
        in_specs=(P("tm", "rows", None, None), P(), P(), P(), P(), P(), P(), P(), P()),
        out_specs=P("tm", "rows", None, None),
        check_vma=False,
    )
```

```python
import functools

import jax
import jax.numpy as jnp
from jax import lax
from jax.experimental import pallas as pl
from jax.experimental.pallas import tpu as pltpu
from jax.sharding import PartitionSpec as P

F32 = jnp.float32
BF16 = jnp.bfloat16
MESH = pl.DeviceIdType.MESH
COLS = 128
UNIT = 8
PER_ROW = COLS // UNIT


def rms_norm(wide, gain):
    scale = lax.rsqrt(jnp.mean(wide * wide, axis=-1, keepdims=True) + 1e-06)
    return wide * scale * gain


def silu(v):
    return v / (1.0 + jnp.exp(-v))


def column_sum(total):
    width, chans = (COLS - UNIT, total.shape[1] // 3)
    left = pltpu.roll(total[:, :chans], 1, 0)
    right = pltpu.roll(total[:, 2 * chans :], COLS - 1, 0)
    return (left + total[:, chans : 2 * chans] + right)[:width]


def padded(value):
    return jnp.concatenate([value, jnp.zeros((COLS - value.shape[0], value.shape[1]), F32)], axis=0)


def kernel(
    steps,
    blocks,
    video_hbm,
    norm_gain_hbm,
    first_hbm,
    second_hbm,
    attn_gain_hbm,
    query_hbm,
    key_hbm,
    value_hbm,
    out_hbm,
    result_ref,
    video,
    norm_gain,
    first,
    second,
    attn_gain,
    query_w,
    key_w,
    value_w,
    out_w,
    act,
    mid,
    acc,
    hidden,
    gathered,
    answer,
    returned,
    relay,
    load_sem,
    halo_send,
    halo_recv,
    relay_send,
    relay_recv,
    swap_send,
    swap_recv,
):
    t, r = (lax.axis_index("tm"), lax.axis_index("rows"))
    chans = video.shape[-1]
    loads = [
        pltpu.make_async_copy(src, dst, load_sem.at[i])
        for i, (src, dst) in enumerate(
            [
                (video_hbm, video),
                (norm_gain_hbm, norm_gain),
                (first_hbm, first),
                (second_hbm, second),
                (attn_gain_hbm, attn_gain),
                (query_hbm, query_w),
                (key_hbm, key_w),
                (value_hbm, value_w),
                (out_hbm, out_w),
            ]
        )
    ]
    for load in loads:
        load.start()

    has_next, has_prev = (t < steps - 1, t > 0)
    has_above, has_below = (r < blocks - 1, r > 0)

    barrier = pltpu.get_barrier_semaphore()

    def greet(j, _):
        peer = lax.rem(t + j, steps)
        pl.semaphore_signal(barrier, inc=1, device_id={"tm": peer, "rows": r}, device_id_type=MESH)
        return 0

    lax.fori_loop(1, steps, greet, 0)

    met = steps - 1
    for side, there in ((1, has_above), (-1, has_below)):
        for shift, then in ((0, True), (1, has_next), (-1, has_prev)):
            present = there if shift == 0 else there & then
            peer = {"tm": t + shift, "rows": r + side}
            met = met + present.astype(jnp.int32)

            @pl.when(present)
            def _(peer=peer):
                pl.semaphore_signal(barrier, inc=1, device_id=peer, device_id_type=MESH)

    outer = (lax.rem(r, 4) == 0) | (lax.rem(r, 4) == 3)
    mirror = r + 3 - 6 * (lax.rem(r, 4) == 3).astype(jnp.int32)
    relays = [(t, r + 4, outer & (r < blocks - 4)), (t, r - 4, outer & (r > 3))]
    relays += [
        (t + shift, mirror, outer & then)
        for shift, then in ((0, True), (1, has_next), (-1, has_prev))
    ]
    for to_t, to_r, present in relays:
        met = met + present.astype(jnp.int32)

        @pl.when(present)
        def _(to_t=to_t, to_r=to_r):
            pl.semaphore_signal(
                barrier, inc=1, device_id={"tm": to_t, "rows": to_r}, device_id_type=MESH
            )

    flip = (lax.rem(r, 4) < 2).astype(jnp.int32)

    def place(q):
        return q + flip * (3 - 2 * q)

    def line(q):
        return q + 2 + flip * (3 - 2 * q)

    def tap(b):
        return b + flip * (2 - 2 * b)

    for field in (act, mid):

        @pl.when(t == 0)
        def _(field=field):
            field[0:2] = jnp.zeros((2,) + field.shape[1:], BF16)

        @pl.when(r == 0)
        def _(field=field):
            for frame in range(4):
                field[frame, 1] = jnp.zeros((COLS, chans), BF16)

        @pl.when(r == blocks - 1)
        def _(field=field):
            for frame in range(4):
                field[frame, 6] = jnp.zeros((COLS, chans), BF16)

    loads[0].wait()
    loads[1].wait()
    gain = norm_gain[...].astype(F32)
    for frame in range(2):
        for row in range(4):
            wide = video[frame, row].astype(F32)
            act[frame + 2, row + 2] = padded(silu(rms_norm(wide, gain))).astype(BF16)

    pl.semaphore_wait(barrier, met)

    def halo(which, field, slots, src, dst, device):
        return pltpu.make_async_remote_copy(
            src_ref=field.at[src],
            dst_ref=field.at[dst],
            send_sem=halo_send.at[which, slots[0]],
            recv_sem=halo_recv.at[which, slots[1]],
            device_id=device,
            device_id_type=MESH,
        )

    own, past = (pl.ds(2, 2), pl.ds(0, 2))
    has_far = jnp.where(flip == 1, has_below, has_above)
    slow, fast = (has_far & outer, has_far & ~outer)
    relaying = outer & jnp.where(flip == 1, r < blocks - 4, r > 3)

    def copies(which, field):
        next_t = jnp.minimum(t + 1, steps - 1)
        near_r = jnp.clip(r - 1 + 2 * flip, 0, blocks - 1)
        far_r = jnp.clip(r + 1 - 2 * flip, 0, blocks - 1)
        later, near, far, next_near, next_far = (
            {"tm": a, "rows": b}
            for a, b in ((next_t, r), (t, near_r), (t, far_r), (next_t, near_r), (next_t, far_r))
        )
        near_land, far_land = (6 - 5 * flip, 1 + 5 * flip)
        far_in, far_in2 = (line(4), line(5))
        inner = pl.ds(3, 2)
        return {
            "inner": halo(which, field, (0, 0), (own, inner), (past, inner), later),
            "first": halo(which, field, (1, 1), (own, line(0)), (past, line(0)), later),
            "last": halo(which, field, (2, 2), (own, line(3)), (past, line(3)), later),
            "to_near": halo(which, field, (3, 4 - flip), (own, line(0)), (own, near_land), near),
            "to_far": halo(which, field, (4, 3 + flip), (own, line(3)), (own, far_land), far),
            "diag_near": halo(
                which, field, (5, 6 - flip), (own, line(0)), (past, near_land), next_near
            ),
            "diag_far": halo(
                which, field, (6, 5 + flip), (own, line(3)), (past, far_land), next_far
            ),
            "from_near": halo(which, field, (3, 3 + flip), (own, line(0)), (own, line(-1)), near),
            "from_far": halo(which, field, (4, 4 - flip), (own, line(3)), (own, far_in), far),
            "past_near": halo(which, field, (5, 5 + flip), (own, line(0)), (past, line(-1)), later),
            "past_far": halo(which, field, (6, 6 - flip), (own, line(3)), (past, far_in), later),
            "from_far2": halo(which, field, (8, 7), (own, line(2)), (own, far_in2), far),
            "past_far2": halo(which, field, (8, 8), (own, line(2)), (past, far_in2), later),
            "beyond": halo(which, field, (9, 8), (own, far_in), (past, far_in), later),
        }

    def across(i):
        return pltpu.make_async_remote_copy(
            src_ref=act.at[own, line(3 - i)],
            dst_ref=relay.at[i],
            send_sem=relay_send.at[i],
            recv_sem=relay_recv.at[i],
            device_id={"tm": t, "rows": jnp.clip(r + 4 - 8 * flip, 0, blocks - 1)},
            device_id_type=MESH,
        )

    def relayed(i, later):
        return pltpu.make_async_remote_copy(
            src_ref=relay.at[i],
            dst_ref=act.at[past if later else own, 7 * flip if i else 1 + 5 * flip],
            send_sem=relay_send.at[2 + 2 * i + later],
            recv_sem=halo_recv.at[0, 7 + later if i else (5 if later else 3) + flip],
            device_id={
                "tm": jnp.minimum(t + later, steps - 1),
                "rows": jnp.clip(mirror, 0, blocks - 1),
            },
            device_id_type=MESH,
        )

    def when(flag, action):
        pl.when(flag)(action)

    def pass_on(i):
        when(relaying, across(i).wait_recv)
        when(relaying, relayed(i, 0).start)
        when(relaying & has_next, relayed(i, 1).start)

    def product(field, weight, frame, early, rows, span):
        pairs = [(a, b) for a in early for b in span]
        cells = jnp.concatenate(
            [
                jnp.concatenate([field[frame + a, line(q + b - 1)] for q in rows], axis=0)
                for a, b in pairs
            ],
            axis=1,
        )
        taps = jnp.concatenate(
            [
                jnp.concatenate([weight[a, tap(b), e] for e in range(3)], axis=1)
                for a, b in pairs
            ],
            axis=0,
        )
        return jnp.dot(cells, taps, preferred_element_type=F32)

    def part(total, i):
        return total[i * COLS : (i + 1) * COLS]

    every = (0, 1, 2)
    groups = (((1, 2), every), ((0,), (1, 2)), ((3,), (0, 1)))

    def to_mid(frame, q, total):
        mid[frame + 2, line(q)] = padded(silu(column_sum(total))).astype(BF16)

    def to_hidden(q, totals):
        one, two = (
            padded(video[frame, place(q)].astype(F32) + column_sum(total)).reshape(
                PER_ROW, UNIT, chans
            )
            for frame, total in enumerate(totals)
        )
        hidden[q] = jnp.concatenate([one, two], axis=1).astype(BF16)

    parity = lax.rem(t, 2)

    def peer_copy(src, dst, send, recv, peer):
        return pltpu.make_async_remote_copy(
            src_ref=src,
            dst_ref=dst,
            send_sem=send,
            recv_sem=recv,
            device_id={"tm": peer, "rows": r},
            device_id_type=MESH,
        )

    def scatter_all():
        def body(j, _):
            peer = lax.rem(t + j, steps)
            peer_copy(
                hidden.at[peer // PER_ROW, lax.rem(peer, PER_ROW)],
                gathered.at[0, t],
                swap_send.at[0, 0],
                swap_recv.at[0, 0],
                peer,
            ).start()
            return 0

        lax.fori_loop(1, steps, body, 0)
        pltpu.make_async_copy(
            hidden.at[t // PER_ROW, lax.rem(t, PER_ROW)], gathered.at[0, t], swap_recv.at[0, 0]
        ).start()

    def scatter_half(odd):
        def send(j):
            spot = lax.rem(t // 2 + j, PER_ROW)
            peer_copy(
                hidden.at[2 + odd, spot],
                gathered.at[1, t],
                swap_send.at[0, 1 + odd],
                swap_recv.at[0, 1],
                2 * spot + odd,
            ).start()

        def body(j, _):
            send(j)
            return 0

        lax.fori_loop(1, PER_ROW, body, 0)
        pl.when(parity != odd)(lambda: send(0))
        pl.when(parity == odd)(
            pltpu.make_async_copy(
                hidden.at[2 + odd, t // 2], gathered.at[1, t], swap_recv.at[0, 1]
            ).start
        )

    def attend(slot):
        pltpu.make_async_copy(gathered.at[slot], gathered.at[slot], swap_recv.at[0, slot]).wait()
        cells = steps * 2 * UNIT
        wide = gathered[slot].reshape(cells, chans).astype(F32)
        normed = rms_norm(wide, attn_gain[...].astype(F32)).astype(BF16)
        joined = jnp.concatenate([query_w[...], key_w[...], value_w[...]], axis=1)
        projected = jnp.dot(normed, joined, preferred_element_type=F32).astype(BF16)
        query = projected[:, :chans]
        key = projected[:, chans : 2 * chans]
        value = projected[:, 2 * chans :]
        tile = 128
        spot = lax.broadcasted_iota(jnp.int32, (tile, tile), 0)
        other = lax.broadcasted_iota(jnp.int32, (tile, tile), 1)
        same = lax.rem(spot, UNIT) == lax.rem(other, UNIT)
        causal = same & (other <= spot)
        root = 1.0 / jnp.sqrt(F32(chans))
        for i in range(cells // tile):
            rows = slice(i * tile, (i + 1) * tile)
            scores = (
                lax.dot_general(
                    query[rows],
                    key[: (i + 1) * tile],
                    (((1,), (1,)), ((), ())),
                    preferred_element_type=F32,
                )
                * root
            )
            tiles = [
                jnp.where(
                    causal if j == i else same, scores[:, j * tile : (j + 1) * tile], F32(-1e30)
                )
                for j in range(i + 1)
            ]
            top = jnp.max(functools.reduce(jnp.maximum, tiles), axis=1, keepdims=True)
            weights = [jnp.exp(one - top) for one in tiles]
            total = jnp.sum(functools.reduce(jnp.add, weights), axis=1, keepdims=True)
            mixed = jnp.dot(
                jnp.concatenate([one.astype(BF16) for one in weights], axis=1),
                value[: (i + 1) * tile],
                preferred_element_type=F32,
            )
            mixed = (mixed / total).astype(BF16)
            shown = wide[rows] + jnp.dot(mixed, out_w[...], preferred_element_type=F32)
            count = tile // (2 * UNIT)
            answer[slot, i * count : (i + 1) * count] = shown.astype(BF16).reshape(
                count, 2 * UNIT, chans
            )
        if slot == 0:
            home = returned.at[t // PER_ROW, lax.rem(t, PER_ROW)]
            arrived = swap_recv.at[1, 0]
        else:
            home = returned.at[2 + parity, t // 2]
            arrived = swap_recv.at[1, 1 + parity]

        def body(j, _):
            peer = lax.rem(t + j, steps)
            peer_copy(answer.at[slot, peer], home, swap_send.at[1, slot], arrived, peer).start()
            return 0

        lax.fori_loop(1, steps, body, 0)
        pltpu.make_async_copy(answer.at[slot, t], home, arrived).start()

    def collect(index, rows):
        block = returned.at[pl.ds(rows[0], len(rows))]
        pltpu.make_async_copy(block, block, swap_recv.at[1, index]).wait()
        for q in rows:
            units = returned[q].astype(F32)
            for frame in range(2):
                cols = units[:, frame * UNIT : (frame + 1) * UNIT].reshape(COLS, chans)
                result_ref[frame, place(q)] = cols[: COLS - UNIT].astype(BF16)

    one, two = (copies(0, act), copies(1, mid))
    when(slow, across(0).start)
    when(fast, one["to_far"].start)
    one["to_near"].start()
    when(has_next, one["diag_near"].start)
    when(has_next & fast, one["diag_far"].start)
    when(slow, across(1).start)
    for name in ("inner", "first", "last"):
        when(has_next, one[name].start)
    loads[2].wait()
    for frame in range(2):
        for rows, span in groups:
            total = product(act, first, frame, range(2 - frame, 3), rows, span)
            for i, q in enumerate(rows):
                acc[frame, q] = part(total, i)
    for name in ("inner", "first", "last"):
        when(has_prev, one[name].wait_recv)
    for rows, span in groups:
        for frame in range(2):
            total = product(act, first, frame, range(0, 2 - frame), rows, span)
            for i, q in enumerate(rows):
                if len(rows) == 2:
                    to_mid(frame, q, acc[frame, q] + part(total, i))
                else:
                    acc[frame, q] += part(total, i)
        if len(rows) == 2:
            when(has_next, two["inner"].start)

    def edge(field, weight, q):
        return [
            acc[frame, q] + product(field, weight, frame, every, (q,), (0,) if q == 0 else (2,))
            for frame in range(2)
        ]

    one["from_near"].wait_recv()
    when(has_prev, one["past_near"].wait_recv)
    for frame, total in enumerate(edge(act, first, 0)):
        to_mid(frame, 0, total)
    two["to_near"].start()
    when(has_next, two["diag_near"].start)
    when(has_next, two["first"].start)
    pass_on(0)
    when(has_far, one["from_far"].wait_recv)
    when(has_prev & has_far, one["past_far"].wait_recv)
    for frame, total in enumerate(edge(act, first, 3)):
        to_mid(frame, 3, total)
    when(fast, two["to_far"].start)
    when(has_next & fast, two["diag_far"].start)
    when(has_next, two["last"].start)

    loads[3].wait()
    for name in ("inner", "first"):
        when(has_prev, two[name].wait_recv)
    to_hidden(1, [product(mid, second, frame, every, (1,), every) for frame in range(2)])
    for frame in range(2):
        acc[frame, 0] = product(mid, second, frame, every, (0,), (1, 2))
    two["from_near"].wait_recv()
    when(has_prev, two["past_near"].wait_recv)
    to_hidden(0, edge(mid, second, 0))
    scatter_all()

    pass_on(1)

    @pl.when(slow)
    def _():
        one["from_far2"].wait_recv()
        when(has_prev, one["past_far2"].wait_recv)
        for frame in range(2):
            to_mid(frame, 4, product(act, first, frame, every, (4,), every))
        when(has_next, two["beyond"].start)

    when(has_prev, two["last"].wait_recv)
    to_hidden(2, [product(mid, second, frame, every, (2,), every) for frame in range(2)])
    scatter_half(0)
    for frame in range(2):
        acc[frame, 3] = product(mid, second, frame, every, (3,), (0, 1))
    when(fast, two["from_far"].wait_recv)
    when(has_prev & fast, two["past_far"].wait_recv)
    when(has_prev & slow, two["beyond"].wait_recv)
    to_hidden(3, edge(mid, second, 3))
    scatter_half(1)

    for load in loads[4:]:
        load.wait()
    attend(0)
    attend(1)
    collect(0, (0, 1))
    collect(1, (2,))
    collect(2, (3,))

    for copy in (one, two):
        copy["to_near"].wait_send()
        for name in ("inner", "first", "last", "diag_near"):
            when(has_next, copy[name].wait_send)
        when(has_next & fast, copy["diag_far"].wait_send)
        when(fast, copy["to_far"].wait_send)
    when(has_next & slow, two["beyond"].wait_send)
    for i in range(2):
        when(slow, across(i).wait_send)
        when(relaying, relayed(i, 0).wait_send)
        when(relaying & has_next, relayed(i, 1).wait_send)

    def gone(count, sem):
        sent = gathered.at[0, pl.ds(0, count)]
        pltpu.make_async_copy(sent, sent, sem).wait()

    gone(steps - 1, swap_send.at[0, 0])
    for odd in range(2):
        pl.when(parity == odd)(lambda odd=odd: gone(PER_ROW - 1, swap_send.at[0, 1 + odd]))
        pl.when(parity != odd)(lambda odd=odd: gone(PER_ROW, swap_send.at[0, 1 + odd]))
    for slot in range(2):
        gone(steps - 1, swap_send.at[1, slot])


def local(video, norm_gain, first, second, attn_gain, query_w, key_w, value_w, out_w):
    steps, blocks = (lax.axis_size("tm"), lax.axis_size("rows"))
    frames, height, width, chans = video.shape
    anywhere = pl.BlockSpec(memory_space=pl.ANY)
    square = (chans, chans)
    return pl.pallas_call(
        functools.partial(kernel, steps, blocks),
        out_shape=jax.ShapeDtypeStruct(video.shape, video.dtype),
        in_specs=[anywhere] * 9,
        out_specs=pl.BlockSpec(memory_space=pltpu.VMEM),
        scratch_shapes=[
            pltpu.VMEM(video.shape, BF16),
            pltpu.VMEM((1, chans), BF16),
            pltpu.VMEM((3, 3, 3) + square, BF16),
            pltpu.VMEM((3, 3, 3) + square, BF16),
            pltpu.VMEM((1, chans), BF16),
            pltpu.VMEM(square, BF16),
            pltpu.VMEM(square, BF16),
            pltpu.VMEM(square, BF16),
            pltpu.VMEM(square, BF16),
            pltpu.VMEM((4, 8, COLS, chans), BF16),
            pltpu.VMEM((4, 8, COLS, chans), BF16),
            pltpu.VMEM((2, 4, COLS, 3 * chans), F32),
            pltpu.VMEM((4, PER_ROW, 2 * UNIT, chans), BF16),
            pltpu.VMEM((2, steps, 2 * UNIT, chans), BF16),
            pltpu.VMEM((2, steps, 2 * UNIT, chans), BF16),
            pltpu.VMEM((4, PER_ROW, 2 * UNIT, chans), BF16),
            pltpu.VMEM((2, 2, COLS, chans), BF16),
            pltpu.SemaphoreType.DMA((9,)),
            pltpu.SemaphoreType.DMA((2, 10)),
            pltpu.SemaphoreType.DMA((2, 9)),
            pltpu.SemaphoreType.DMA((6,)),
            pltpu.SemaphoreType.DMA((2,)),
            pltpu.SemaphoreType.DMA((2, 3)),
            pltpu.SemaphoreType.DMA((2, 3)),
        ],
        compiler_params=pltpu.CompilerParams(
            collective_id=0, has_side_effects=True, vmem_limit_bytes=56 * 1024 * 1024
        ),
    )(
        video,
        norm_gain.reshape(1, chans),
        first,
        second,
        attn_gain.reshape(1, chans),
        query_w,
        key_w,
        value_w,
        out_w,
    )


def solution(mesh):
    return jax.shard_map(
        local,
        mesh=mesh,
        in_specs=(P("tm", "rows", None, None), P(), P(), P(), P(), P(), P(), P(), P()),
        out_specs=P("tm", "rows", None, None),
        check_vma=False,
    )
```

```python
import functools

import jax
import jax.numpy as jnp
from jax import lax
from jax.experimental import pallas as pl
from jax.experimental.pallas import tpu as pltpu
from jax.sharding import PartitionSpec as P

F32 = jnp.float32
BF16 = jnp.bfloat16
MESH = pl.DeviceIdType.MESH
COLS = 128
UNIT = 8
PER_ROW = COLS // UNIT


def rms_norm(wide, gain):
    scale = lax.rsqrt(jnp.mean(wide * wide, axis=-1, keepdims=True) + 1e-06)
    return wide * scale * gain


def silu(v):
    return v / (1.0 + jnp.exp(-v))


def column_sum(total):
    width, chans = (COLS - UNIT, total.shape[1] // 3)
    left = pltpu.roll(total[:, :chans], 1, 0)
    right = pltpu.roll(total[:, 2 * chans :], COLS - 1, 0)
    return (left + total[:, chans : 2 * chans] + right)[:width]


def padded(value):
    return jnp.concatenate([value, jnp.zeros((COLS - value.shape[0], value.shape[1]), F32)], axis=0)


def kernel(
    steps,
    blocks,
    video_hbm,
    norm_gain_hbm,
    first_hbm,
    second_hbm,
    attn_gain_hbm,
    query_hbm,
    key_hbm,
    value_hbm,
    out_hbm,
    result_ref,
    video,
    norm_gain,
    first,
    second,
    attn_gain,
    query_w,
    key_w,
    value_w,
    out_w,
    act,
    mid,
    acc,
    hidden,
    gathered,
    answer,
    returned,
    load_sem,
    halo_send,
    halo_recv,
    swap_send,
    swap_recv,
):
    t, r = (lax.axis_index("tm"), lax.axis_index("rows"))
    chans = video.shape[-1]
    loads = [
        pltpu.make_async_copy(src, dst, load_sem.at[i])
        for i, (src, dst) in enumerate(
            [
                (video_hbm, video),
                (norm_gain_hbm, norm_gain),
                (first_hbm, first),
                (second_hbm, second),
                (attn_gain_hbm, attn_gain),
                (query_hbm, query_w),
                (key_hbm, key_w),
                (value_hbm, value_w),
                (out_hbm, out_w),
            ]
        )
    ]
    for load in loads:
        load.start()

    has_next, has_prev = (t < steps - 1, t > 0)
    has_above, has_below = (r < blocks - 1, r > 0)

    barrier = pltpu.get_barrier_semaphore()

    def greet(j, _):
        peer = lax.rem(t + j, steps)
        pl.semaphore_signal(barrier, inc=1, device_id={"tm": peer, "rows": r}, device_id_type=MESH)
        return 0

    lax.fori_loop(1, steps, greet, 0)

    met = steps - 1
    for side, there in ((1, has_above), (-1, has_below)):
        for shift, then in ((0, True), (1, has_next), (-1, has_prev)):
            present = there if shift == 0 else there & then
            peer = {"tm": t + shift, "rows": r + side}
            met = met + present.astype(jnp.int32)

            @pl.when(present)
            def _(peer=peer):
                pl.semaphore_signal(barrier, inc=1, device_id=peer, device_id_type=MESH)

    flip = (lax.rem(r, 4) < 2).astype(jnp.int32)

    def place(q):
        return q + flip * (3 - 2 * q)

    def line(q):
        return q + 2 + flip * (3 - 2 * q)

    def tap(b):
        return b + flip * (2 - 2 * b)

    for field in (act, mid):

        @pl.when(t == 0)
        def _(field=field):
            field[0:2] = jnp.zeros((2,) + field.shape[1:], BF16)

        @pl.when(r == 0)
        def _(field=field):
            for frame in range(4):
                field[frame, 1] = jnp.zeros((COLS, chans), BF16)

        @pl.when(r == blocks - 1)
        def _(field=field):
            for frame in range(4):
                field[frame, 6] = jnp.zeros((COLS, chans), BF16)

    loads[0].wait()
    loads[1].wait()
    gain = norm_gain[...].astype(F32)
    for frame in range(2):
        for row in range(4):
            wide = video[frame, row].astype(F32)
            act[frame + 2, row + 2] = padded(silu(rms_norm(wide, gain))).astype(BF16)

    pl.semaphore_wait(barrier, met)

    def halo(which, field, slots, src, dst, device):
        return pltpu.make_async_remote_copy(
            src_ref=field.at[src],
            dst_ref=field.at[dst],
            send_sem=halo_send.at[which, slots[0]],
            recv_sem=halo_recv.at[which, slots[1]],
            device_id=device,
            device_id_type=MESH,
        )

    own, past = (pl.ds(2, 2), pl.ds(0, 2))
    has_far = jnp.where(flip == 1, has_below, has_above)
    slow = has_far & ((lax.rem(r, 4) == 0) | (lax.rem(r, 4) == 3))
    fast = has_far & ~((lax.rem(r, 4) == 0) | (lax.rem(r, 4) == 3))

    def copies(which, field):
        next_t = jnp.minimum(t + 1, steps - 1)
        near_r = jnp.clip(r - 1 + 2 * flip, 0, blocks - 1)
        far_r = jnp.clip(r + 1 - 2 * flip, 0, blocks - 1)
        later, near, far, next_near, next_far = (
            {"tm": a, "rows": b}
            for a, b in ((next_t, r), (t, near_r), (t, far_r), (next_t, near_r), (next_t, far_r))
        )
        near_land, far_land = (6 - 5 * flip, 1 + 5 * flip)
        far_in = line(4)
        inner = pl.ds(3, 2)
        return {
            "inner": halo(which, field, (0, 0), (own, inner), (past, inner), later),
            "first": halo(which, field, (1, 1), (own, line(0)), (past, line(0)), later),
            "last": halo(which, field, (2, 2), (own, line(3)), (past, line(3)), later),
            "to_near": halo(which, field, (3, 4 - flip), (own, line(0)), (own, near_land), near),
            "to_far": halo(which, field, (4, 3 + flip), (own, line(3)), (own, far_land), far),
            "diag_near": halo(
                which, field, (5, 6 - flip), (own, line(0)), (past, near_land), next_near
            ),
            "diag_far": halo(
                which, field, (6, 5 + flip), (own, line(3)), (past, far_land), next_far
            ),
            "from_near": halo(which, field, (3, 3 + flip), (own, line(0)), (own, line(-1)), near),
            "from_far": halo(which, field, (4, 4 - flip), (own, line(3)), (own, far_in), far),
            "past_near": halo(which, field, (5, 5 + flip), (own, line(0)), (past, line(-1)), later),
            "on_far": halo(which, field, (7, 6 - flip), (own, far_in), (past, far_in), later),
        }

    def when(flag, action):
        pl.when(flag)(action)

    def product(field, weight, frame, early, rows, span):
        pairs = [(a, b) for a in early for b in span]
        cells = jnp.concatenate(
            [
                jnp.concatenate([field[frame + a, line(q + b - 1)] for q in rows], axis=0)
                for a, b in pairs
            ],
            axis=1,
        )
        taps = jnp.concatenate(
            [
                jnp.concatenate([weight[a, tap(b), e] for e in range(3)], axis=1)
                for a, b in pairs
            ],
            axis=0,
        )
        return jnp.dot(cells, taps, preferred_element_type=F32)

    def part(total, i):
        return total[i * COLS : (i + 1) * COLS]

    every = (0, 1, 2)
    groups = (((1, 2), every), ((0,), (1, 2)), ((3,), (0, 1)))

    def to_mid(frame, q, total):
        mid[frame + 2, line(q)] = padded(silu(column_sum(total))).astype(BF16)

    def to_hidden(q, totals):
        one, two = (
            padded(video[frame, place(q)].astype(F32) + column_sum(total)).reshape(
                PER_ROW, UNIT, chans
            )
            for frame, total in enumerate(totals)
        )
        hidden[q] = jnp.concatenate([one, two], axis=1).astype(BF16)

    parity = lax.rem(t, 2)

    def peer_copy(src, dst, send, recv, peer):
        return pltpu.make_async_remote_copy(
            src_ref=src,
            dst_ref=dst,
            send_sem=send,
            recv_sem=recv,
            device_id={"tm": peer, "rows": r},
            device_id_type=MESH,
        )

    def scatter_all():
        def body(j, _):
            peer = lax.rem(t + j, steps)
            peer_copy(
                hidden.at[peer // PER_ROW, lax.rem(peer, PER_ROW)],
                gathered.at[0, t],
                swap_send.at[0, 0],
                swap_recv.at[0, 0],
                peer,
            ).start()
            return 0

        lax.fori_loop(1, steps, body, 0)
        pltpu.make_async_copy(
            hidden.at[t // PER_ROW, lax.rem(t, PER_ROW)], gathered.at[0, t], swap_recv.at[0, 0]
        ).start()

    def scatter_half(odd):
        def send(j):
            spot = lax.rem(t // 2 + j, PER_ROW)
            peer_copy(
                hidden.at[2 + odd, spot],
                gathered.at[1, t],
                swap_send.at[0, 1 + odd],
                swap_recv.at[0, 1],
                2 * spot + odd,
            ).start()

        def body(j, _):
            send(j)
            return 0

        lax.fori_loop(1, PER_ROW, body, 0)
        pl.when(parity != odd)(lambda: send(0))
        pl.when(parity == odd)(
            pltpu.make_async_copy(
                hidden.at[2 + odd, t // 2], gathered.at[1, t], swap_recv.at[0, 1]
            ).start
        )

    def attend(slot):
        pltpu.make_async_copy(gathered.at[slot], gathered.at[slot], swap_recv.at[0, slot]).wait()
        cells = steps * 2 * UNIT
        wide = gathered[slot].reshape(cells, chans).astype(F32)
        normed = rms_norm(wide, attn_gain[...].astype(F32)).astype(BF16)
        joined = jnp.concatenate([query_w[...], key_w[...], value_w[...]], axis=1)
        projected = jnp.dot(normed, joined, preferred_element_type=F32).astype(BF16)
        query = projected[:, :chans]
        key = projected[:, chans : 2 * chans]
        value = projected[:, 2 * chans :]
        tile = 128
        spot = lax.broadcasted_iota(jnp.int32, (tile, tile), 0)
        other = lax.broadcasted_iota(jnp.int32, (tile, tile), 1)
        same = lax.rem(spot, UNIT) == lax.rem(other, UNIT)
        causal = same & (other <= spot)
        root = 1.0 / jnp.sqrt(F32(chans))
        for i in range(cells // tile):
            rows = slice(i * tile, (i + 1) * tile)
            scores = (
                lax.dot_general(
                    query[rows],
                    key[: (i + 1) * tile],
                    (((1,), (1,)), ((), ())),
                    preferred_element_type=F32,
                )
                * root
            )
            tiles = [
                jnp.where(
                    causal if j == i else same, scores[:, j * tile : (j + 1) * tile], F32(-1e30)
                )
                for j in range(i + 1)
            ]
            top = jnp.max(functools.reduce(jnp.maximum, tiles), axis=1, keepdims=True)
            weights = [jnp.exp(one - top) for one in tiles]
            total = jnp.sum(functools.reduce(jnp.add, weights), axis=1, keepdims=True)
            mixed = jnp.dot(
                jnp.concatenate([one.astype(BF16) for one in weights], axis=1),
                value[: (i + 1) * tile],
                preferred_element_type=F32,
            )
            mixed = (mixed / total).astype(BF16)
            shown = wide[rows] + jnp.dot(mixed, out_w[...], preferred_element_type=F32)
            count = tile // (2 * UNIT)
            answer[slot, i * count : (i + 1) * count] = shown.astype(BF16).reshape(
                count, 2 * UNIT, chans
            )
        if slot == 0:
            home = returned.at[t // PER_ROW, lax.rem(t, PER_ROW)]
            arrived = swap_recv.at[1, 0]
        else:
            home = returned.at[2 + parity, t // 2]
            arrived = swap_recv.at[1, 1 + parity]

        def body(j, _):
            peer = lax.rem(t + j, steps)
            peer_copy(answer.at[slot, peer], home, swap_send.at[1, slot], arrived, peer).start()
            return 0

        lax.fori_loop(1, steps, body, 0)
        pltpu.make_async_copy(answer.at[slot, t], home, arrived).start()

    def collect(index, rows):
        block = returned.at[pl.ds(rows[0], len(rows))]
        pltpu.make_async_copy(block, block, swap_recv.at[1, index]).wait()
        for q in rows:
            units = returned[q].astype(F32)
            for frame in range(2):
                cols = units[:, frame * UNIT : (frame + 1) * UNIT].reshape(COLS, chans)
                result_ref[frame, place(q)] = cols[: COLS - UNIT].astype(BF16)

    one, two = (copies(0, act), copies(1, mid))
    when(has_far, one["to_far"].start)
    one["to_near"].start()
    when(has_next, one["diag_near"].start)
    when(has_next & fast, one["diag_far"].start)
    for name in ("inner", "first", "last"):
        when(has_next, one[name].start)
    loads[2].wait()
    for frame in range(2):
        for rows, span in groups:
            total = product(act, first, frame, range(2 - frame, 3), rows, span)
            for i, q in enumerate(rows):
                acc[frame, q] = part(total, i)
    for name in ("inner", "first", "last"):
        when(has_prev, one[name].wait_recv)
    for rows, span in groups:
        for frame in range(2):
            total = product(act, first, frame, range(0, 2 - frame), rows, span)
            for i, q in enumerate(rows):
                if len(rows) == 2:
                    to_mid(frame, q, acc[frame, q] + part(total, i))
                else:
                    acc[frame, q] += part(total, i)
        if len(rows) == 2:
            when(has_next, two["inner"].start)

    def edge(field, weight, q):
        return [
            acc[frame, q] + product(field, weight, frame, every, (q,), (0,) if q == 0 else (2,))
            for frame in range(2)
        ]

    one["from_near"].wait_recv()
    when(has_prev, one["past_near"].wait_recv)
    for frame, total in enumerate(edge(act, first, 0)):
        to_mid(frame, 0, total)
    two["to_near"].start()
    when(has_next, two["diag_near"].start)
    when(has_next, two["first"].start)
    when(has_far, one["from_far"].wait_recv)
    when(has_next & slow, one["on_far"].start)
    when(has_prev & has_far, one["on_far"].wait_recv)
    for frame, total in enumerate(edge(act, first, 3)):
        to_mid(frame, 3, total)
    when(has_far, two["to_far"].start)
    when(has_next & fast, two["diag_far"].start)
    when(has_next, two["last"].start)

    loads[3].wait()
    for name in ("inner", "first"):
        when(has_prev, two[name].wait_recv)
    to_hidden(1, [product(mid, second, frame, every, (1,), every) for frame in range(2)])
    for frame in range(2):
        acc[frame, 0] = product(mid, second, frame, every, (0,), (1, 2))
    two["from_near"].wait_recv()
    when(has_prev, two["past_near"].wait_recv)
    to_hidden(0, edge(mid, second, 0))
    scatter_all()

    when(has_prev, two["last"].wait_recv)
    to_hidden(2, [product(mid, second, frame, every, (2,), every) for frame in range(2)])
    scatter_half(0)
    for frame in range(2):
        acc[frame, 3] = product(mid, second, frame, every, (3,), (0, 1))
    when(has_far, two["from_far"].wait_recv)
    when(has_next & slow, two["on_far"].start)
    when(has_prev & has_far, two["on_far"].wait_recv)
    to_hidden(3, edge(mid, second, 3))
    scatter_half(1)

    for load in loads[4:]:
        load.wait()
    attend(0)
    attend(1)
    collect(0, (0, 1))
    collect(1, (2,))
    collect(2, (3,))

    for copy in (one, two):
        copy["to_near"].wait_send()
        for name in ("inner", "first", "last", "diag_near"):
            when(has_next, copy[name].wait_send)
        when(has_next & fast, copy["diag_far"].wait_send)
    for copy in (one, two):
        when(has_far, copy["to_far"].wait_send)
        when(has_next & slow, copy["on_far"].wait_send)

    def gone(count, sem):
        sent = gathered.at[0, pl.ds(0, count)]
        pltpu.make_async_copy(sent, sent, sem).wait()

    gone(steps - 1, swap_send.at[0, 0])
    for odd in range(2):
        pl.when(parity == odd)(lambda odd=odd: gone(PER_ROW - 1, swap_send.at[0, 1 + odd]))
        pl.when(parity != odd)(lambda odd=odd: gone(PER_ROW, swap_send.at[0, 1 + odd]))
    for slot in range(2):
        gone(steps - 1, swap_send.at[1, slot])


def local(video, norm_gain, first, second, attn_gain, query_w, key_w, value_w, out_w):
    steps, blocks = (lax.axis_size("tm"), lax.axis_size("rows"))
    frames, height, width, chans = video.shape
    anywhere = pl.BlockSpec(memory_space=pl.ANY)
    square = (chans, chans)
    return pl.pallas_call(
        functools.partial(kernel, steps, blocks),
        out_shape=pltpu.VMEM(video.shape, BF16),
        in_specs=[anywhere] * 9,
        out_specs=pl.BlockSpec(memory_space=pltpu.VMEM),
        scratch_shapes=[
            pltpu.VMEM(video.shape, BF16),
            pltpu.VMEM((1, chans), BF16),
            pltpu.VMEM((3, 3, 3) + square, BF16),
            pltpu.VMEM((3, 3, 3) + square, BF16),
            pltpu.VMEM((1, chans), BF16),
            pltpu.VMEM(square, BF16),
            pltpu.VMEM(square, BF16),
            pltpu.VMEM(square, BF16),
            pltpu.VMEM(square, BF16),
            pltpu.VMEM((4, 8, COLS, chans), BF16),
            pltpu.VMEM((4, 8, COLS, chans), BF16),
            pltpu.VMEM((2, 4, COLS, 3 * chans), F32),
            pltpu.VMEM((4, PER_ROW, 2 * UNIT, chans), BF16),
            pltpu.VMEM((2, steps, 2 * UNIT, chans), BF16),
            pltpu.VMEM((2, steps, 2 * UNIT, chans), BF16),
            pltpu.VMEM((4, PER_ROW, 2 * UNIT, chans), BF16),
            pltpu.SemaphoreType.DMA((9,)),
            pltpu.SemaphoreType.DMA((2, 10)),
            pltpu.SemaphoreType.DMA((2, 10)),
            pltpu.SemaphoreType.DMA((2, 3)),
            pltpu.SemaphoreType.DMA((2, 3)),
        ],
        compiler_params=pltpu.CompilerParams(
            collective_id=0, has_side_effects=True, vmem_limit_bytes=56 * 1024 * 1024
        ),
    )(
        video,
        norm_gain.reshape(1, chans),
        first,
        second,
        attn_gain.reshape(1, chans),
        query_w,
        key_w,
        value_w,
        out_w,
    )


def solution(mesh):
    return jax.shard_map(
        local,
        mesh=mesh,
        in_specs=(P("tm", "rows", None, None), P(), P(), P(), P(), P(), P(), P(), P()),
        out_specs=P("tm", "rows", None, None),
        check_vma=False,
    )
```

```python
import functools

import jax
import jax.numpy as jnp
from jax import lax
from jax.experimental import pallas as pl
from jax.experimental.pallas import tpu as pltpu
from jax.sharding import PartitionSpec as P

F32 = jnp.float32
BF16 = jnp.bfloat16
MESH = pl.DeviceIdType.MESH
COLS = 128
UNIT = 8
PER_ROW = COLS // UNIT


def rms_norm(wide, gain):
    scale = lax.rsqrt(jnp.mean(wide * wide, axis=-1, keepdims=True) + 1e-06)
    return wide * scale * gain


def silu(v):
    return v / (1.0 + jnp.exp(-v))


def column_sum(total):
    width, chans = (COLS - UNIT, total.shape[1] // 3)
    left = pltpu.roll(total[:, :chans], 1, 0)
    right = pltpu.roll(total[:, 2 * chans :], COLS - 1, 0)
    return (left + total[:, chans : 2 * chans] + right)[:width]


def padded(value):
    return jnp.concatenate([value, jnp.zeros((COLS - value.shape[0], value.shape[1]), F32)], axis=0)


def kernel(
    steps,
    blocks,
    video_hbm,
    norm_gain_hbm,
    first_hbm,
    second_hbm,
    attn_gain_hbm,
    query_hbm,
    key_hbm,
    value_hbm,
    out_hbm,
    result_ref,
    video,
    norm_gain,
    first,
    second,
    attn_gain,
    query_w,
    key_w,
    value_w,
    out_w,
    act,
    mid,
    acc,
    hidden,
    gathered,
    answer,
    returned,
    load_sem,
    halo_send,
    halo_recv,
    swap_send,
    swap_recv,
):
    t, r = (lax.axis_index("tm"), lax.axis_index("rows"))
    chans = video.shape[-1]
    loads = [
        pltpu.make_async_copy(src, dst, load_sem.at[i])
        for i, (src, dst) in enumerate(
            [
                (video_hbm, video),
                (norm_gain_hbm, norm_gain),
                (first_hbm, first),
                (second_hbm, second),
                (attn_gain_hbm, attn_gain),
                (query_hbm, query_w),
                (key_hbm, key_w),
                (value_hbm, value_w),
                (out_hbm, out_w),
            ]
        )
    ]
    for load in loads:
        load.start()

    has_next, has_prev = (t < steps - 1, t > 0)
    has_above, has_below = (r < blocks - 1, r > 0)

    barrier = pltpu.get_barrier_semaphore()

    def greet(j, _):
        peer = lax.rem(t + j, steps)
        pl.semaphore_signal(barrier, inc=1, device_id={"tm": peer, "rows": r}, device_id_type=MESH)
        return 0

    lax.fori_loop(1, steps, greet, 0)

    met = steps - 1
    for side, there in ((1, has_above), (-1, has_below)):
        for shift, then in ((0, True), (1, has_next), (-1, has_prev)):
            present = there if shift == 0 else there & then
            peer = {"tm": t + shift, "rows": r + side}
            met = met + present.astype(jnp.int32)

            @pl.when(present)
            def _(peer=peer):
                pl.semaphore_signal(barrier, inc=1, device_id=peer, device_id_type=MESH)

    flip = (lax.rem(r, 4) < 2).astype(jnp.int32)

    def place(q):
        return q + flip * (3 - 2 * q)

    def line(q):
        return q + 2 + flip * (3 - 2 * q)

    def tap(b):
        return b + flip * (2 - 2 * b)

    for field in (act, mid):

        @pl.when(t == 0)
        def _(field=field):
            field[0:2] = jnp.zeros((2,) + field.shape[1:], BF16)

        @pl.when(r == 0)
        def _(field=field):
            for frame in range(4):
                field[frame, 1] = jnp.zeros((COLS, chans), BF16)

        @pl.when(r == blocks - 1)
        def _(field=field):
            for frame in range(4):
                field[frame, 6] = jnp.zeros((COLS, chans), BF16)

    loads[0].wait()
    loads[1].wait()
    gain = norm_gain[...].astype(F32)
    for frame in range(2):
        for row in range(4):
            wide = video[frame, row].astype(F32)
            act[frame + 2, row + 2] = padded(silu(rms_norm(wide, gain))).astype(BF16)

    pl.semaphore_wait(barrier, met)

    def halo(which, field, slots, src, dst, device):
        return pltpu.make_async_remote_copy(
            src_ref=field.at[src],
            dst_ref=field.at[dst],
            send_sem=halo_send.at[which, slots[0]],
            recv_sem=halo_recv.at[which, slots[1]],
            device_id=device,
            device_id_type=MESH,
        )

    own, past = (pl.ds(2, 2), pl.ds(0, 2))
    has_far = jnp.where(flip == 1, has_below, has_above)
    slow = has_far & ((lax.rem(r, 4) == 0) | (lax.rem(r, 4) == 3))
    fast = has_far & ~((lax.rem(r, 4) == 0) | (lax.rem(r, 4) == 3))

    def copies(which, field):
        next_t = jnp.minimum(t + 1, steps - 1)
        near_r = jnp.clip(r - 1 + 2 * flip, 0, blocks - 1)
        far_r = jnp.clip(r + 1 - 2 * flip, 0, blocks - 1)
        later, near, far, next_near, next_far = (
            {"tm": a, "rows": b}
            for a, b in ((next_t, r), (t, near_r), (t, far_r), (next_t, near_r), (next_t, far_r))
        )
        near_land, far_land = (6 - 5 * flip, 1 + 5 * flip)
        far_in = line(4)
        inner = pl.ds(3, 2)
        return {
            "inner": halo(which, field, (0, 0), (own, inner), (past, inner), later),
            "first": halo(which, field, (1, 1), (own, line(0)), (past, line(0)), later),
            "last": halo(which, field, (2, 2), (own, line(3)), (past, line(3)), later),
            "to_near": halo(which, field, (3, 4 - flip), (own, line(0)), (own, near_land), near),
            "to_far": halo(which, field, (4, 3 + flip), (own, line(3)), (own, far_land), far),
            "diag_near": halo(
                which, field, (5, 6 - flip), (own, line(0)), (past, near_land), next_near
            ),
            "diag_far": halo(
                which, field, (6, 5 + flip), (own, line(3)), (past, far_land), next_far
            ),
            "from_near": halo(which, field, (3, 3 + flip), (own, line(0)), (own, line(-1)), near),
            "from_far": halo(which, field, (4, 4 - flip), (own, line(3)), (own, far_in), far),
            "past_near": halo(which, field, (5, 5 + flip), (own, line(0)), (past, line(-1)), later),
            "on_far": halo(which, field, (7, 6 - flip), (own, far_in), (past, far_in), later),
        }

    def when(flag, action):
        pl.when(flag)(action)

    def product(field, weight, frame, early, rows, span):
        pairs = [(a, b) for a in early for b in span]
        cells = jnp.concatenate(
            [
                jnp.concatenate([field[frame + a, line(q + b - 1)] for q in rows], axis=0)
                for a, b in pairs
            ],
            axis=1,
        )
        taps = jnp.concatenate(
            [
                jnp.concatenate([weight[a, tap(b), e] for e in range(3)], axis=1)
                for a, b in pairs
            ],
            axis=0,
        )
        return jnp.dot(cells, taps, preferred_element_type=F32)

    def part(total, i):
        return total[i * COLS : (i + 1) * COLS]

    every = (0, 1, 2)
    groups = (((1, 2), every), ((0,), (1, 2)), ((3,), (0, 1)))

    def to_mid(frame, q, total):
        mid[frame + 2, line(q)] = padded(silu(column_sum(total))).astype(BF16)

    def to_hidden(q, totals):
        one, two = (
            padded(video[frame, place(q)].astype(F32) + column_sum(total)).reshape(
                PER_ROW, UNIT, chans
            )
            for frame, total in enumerate(totals)
        )
        hidden[q] = jnp.concatenate([one, two], axis=1).astype(BF16)

    parity = lax.rem(t, 2)
    full = PER_ROW - 1
    works = [lax.rem(t, PER_ROW) < full, t // 2 < full]

    def peer_copy(src, dst, send, recv, peer):
        return pltpu.make_async_remote_copy(
            src_ref=src,
            dst_ref=dst,
            send_sem=send,
            recv_sem=recv,
            device_id={"tm": peer, "rows": r},
            device_id_type=MESH,
        )

    def scatter_all():
        def body(j, _):
            peer = lax.rem(t + j, steps)
            copy = peer_copy(
                hidden.at[peer // PER_ROW, lax.rem(peer, PER_ROW)],
                gathered.at[0, t],
                swap_send.at[0, 0],
                swap_recv.at[0, 0],
                peer,
            )
            pl.when(lax.rem(peer, PER_ROW) < full)(copy.start)
            return 0

        lax.fori_loop(1, steps, body, 0)
        own_unit = pltpu.make_async_copy(
            hidden.at[t // PER_ROW, lax.rem(t, PER_ROW)], gathered.at[0, t], swap_recv.at[0, 0]
        )
        pl.when(works[0])(own_unit.start)

    def scatter_half(odd):
        def send(j):
            spot = lax.rem(t // 2 + j, PER_ROW)
            copy = peer_copy(
                hidden.at[2 + odd, spot],
                gathered.at[1, t],
                swap_send.at[0, 1 + odd],
                swap_recv.at[0, 1],
                2 * spot + odd,
            )
            pl.when(spot < full)(copy.start)

        def body(j, _):
            send(j)
            return 0

        lax.fori_loop(1, PER_ROW, body, 0)
        pl.when(parity != odd)(lambda: send(0))
        pl.when((parity == odd) & works[1])(
            pltpu.make_async_copy(
                hidden.at[2 + odd, t // 2], gathered.at[1, t], swap_recv.at[0, 1]
            ).start
        )

    def attend(slot):
        pltpu.make_async_copy(gathered.at[slot], gathered.at[slot], swap_recv.at[0, slot]).wait()
        cells = steps * 2 * UNIT
        wide = gathered[slot].reshape(cells, chans).astype(F32)
        normed = rms_norm(wide, attn_gain[...].astype(F32)).astype(BF16)
        joined = jnp.concatenate([query_w[...], key_w[...], value_w[...]], axis=1)
        projected = jnp.dot(normed, joined, preferred_element_type=F32).astype(BF16)
        query = projected[:, :chans]
        key = projected[:, chans : 2 * chans]
        value = projected[:, 2 * chans :]
        tile = 128
        spot = lax.broadcasted_iota(jnp.int32, (tile, tile), 0)
        other = lax.broadcasted_iota(jnp.int32, (tile, tile), 1)
        same = lax.rem(spot, UNIT) == lax.rem(other, UNIT)
        causal = same & (other <= spot)
        root = 1.0 / jnp.sqrt(F32(chans))
        for i in range(cells // tile):
            rows = slice(i * tile, (i + 1) * tile)
            scores = (
                lax.dot_general(
                    query[rows],
                    key[: (i + 1) * tile],
                    (((1,), (1,)), ((), ())),
                    preferred_element_type=F32,
                )
                * root
            )
            tiles = [
                jnp.where(
                    causal if j == i else same, scores[:, j * tile : (j + 1) * tile], F32(-1e30)
                )
                for j in range(i + 1)
            ]
            top = jnp.max(functools.reduce(jnp.maximum, tiles), axis=1, keepdims=True)
            weights = [jnp.exp(one - top) for one in tiles]
            total = jnp.sum(functools.reduce(jnp.add, weights), axis=1, keepdims=True)
            mixed = jnp.dot(
                jnp.concatenate([one.astype(BF16) for one in weights], axis=1),
                value[: (i + 1) * tile],
                preferred_element_type=F32,
            )
            mixed = (mixed / total).astype(BF16)
            shown = wide[rows] + jnp.dot(mixed, out_w[...], preferred_element_type=F32)
            count = tile // (2 * UNIT)
            answer[slot, i * count : (i + 1) * count] = shown.astype(BF16).reshape(
                count, 2 * UNIT, chans
            )
        if slot == 0:
            home = returned.at[t // PER_ROW, lax.rem(t, PER_ROW)]
            arrived = swap_recv.at[1, 0]
        else:
            home = returned.at[2 + parity, t // 2]
            arrived = swap_recv.at[1, 1 + parity]

        def body(j, _):
            peer = lax.rem(t + j, steps)
            peer_copy(answer.at[slot, peer], home, swap_send.at[1, slot], arrived, peer).start()
            return 0

        lax.fori_loop(1, steps, body, 0)
        pltpu.make_async_copy(answer.at[slot, t], home, arrived).start()

    def collect(index, rows):
        block = returned.at[pl.ds(rows[0], len(rows)), pl.ds(0, full)]
        pltpu.make_async_copy(block, block, swap_recv.at[1, index]).wait()
        for q in rows:
            units = returned[q, 0:full].astype(F32)
            for frame in range(2):
                cols = units[:, frame * UNIT : (frame + 1) * UNIT].reshape(full * UNIT, chans)
                result_ref[frame, place(q)] = cols.astype(BF16)

    one, two = (copies(0, act), copies(1, mid))
    when(has_far, one["to_far"].start)
    one["to_near"].start()
    when(has_next, one["diag_near"].start)
    when(has_next & fast, one["diag_far"].start)
    for name in ("inner", "first", "last"):
        when(has_next, one[name].start)
    loads[2].wait()
    for frame in range(2):
        for rows, span in groups:
            total = product(act, first, frame, range(2 - frame, 3), rows, span)
            for i, q in enumerate(rows):
                acc[frame, q] = part(total, i)
    for name in ("inner", "first", "last"):
        when(has_prev, one[name].wait_recv)
    for rows, span in groups:
        for frame in range(2):
            total = product(act, first, frame, range(0, 2 - frame), rows, span)
            for i, q in enumerate(rows):
                if len(rows) == 2:
                    to_mid(frame, q, acc[frame, q] + part(total, i))
                else:
                    acc[frame, q] += part(total, i)
        if len(rows) == 2:
            when(has_next, two["inner"].start)

    def edge(field, weight, q):
        return [
            acc[frame, q] + product(field, weight, frame, every, (q,), (0,) if q == 0 else (2,))
            for frame in range(2)
        ]

    one["from_near"].wait_recv()
    when(has_prev, one["past_near"].wait_recv)
    for frame, total in enumerate(edge(act, first, 0)):
        to_mid(frame, 0, total)
    two["to_near"].start()
    when(has_next, two["diag_near"].start)
    when(has_next, two["first"].start)
    when(has_far, one["from_far"].wait_recv)
    when(has_next & slow, one["on_far"].start)
    when(has_prev & has_far, one["on_far"].wait_recv)
    for frame, total in enumerate(edge(act, first, 3)):
        to_mid(frame, 3, total)
    when(has_far, two["to_far"].start)
    when(has_next & fast, two["diag_far"].start)
    when(has_next, two["last"].start)

    loads[3].wait()
    for name in ("inner", "first"):
        when(has_prev, two[name].wait_recv)
    to_hidden(1, [product(mid, second, frame, every, (1,), every) for frame in range(2)])
    for frame in range(2):
        acc[frame, 0] = product(mid, second, frame, every, (0,), (1, 2))
    two["from_near"].wait_recv()
    when(has_prev, two["past_near"].wait_recv)
    to_hidden(0, edge(mid, second, 0))
    scatter_all()

    when(has_prev, two["last"].wait_recv)
    to_hidden(2, [product(mid, second, frame, every, (2,), every) for frame in range(2)])
    scatter_half(0)
    for frame in range(2):
        acc[frame, 3] = product(mid, second, frame, every, (3,), (0, 1))
    when(has_far, two["from_far"].wait_recv)
    when(has_next & slow, two["on_far"].start)
    when(has_prev & has_far, two["on_far"].wait_recv)
    to_hidden(3, edge(mid, second, 3))
    scatter_half(1)

    for load in loads[4:]:
        load.wait()
    for slot in range(2):
        pl.when(works[slot])(lambda slot=slot: attend(slot))
    collect(0, (0, 1))
    collect(1, (2,))
    collect(2, (3,))

    for copy in (one, two):
        copy["to_near"].wait_send()
        for name in ("inner", "first", "last", "diag_near"):
            when(has_next, copy[name].wait_send)
        when(has_next & fast, copy["diag_far"].wait_send)
    for copy in (one, two):
        when(has_far, copy["to_far"].wait_send)
        when(has_next & slow, copy["on_far"].wait_send)

    def gone(count, sem):
        sent = gathered.at[0, pl.ds(0, count)]
        pltpu.make_async_copy(sent, sent, sem).wait()

    for mine, count, sem in (
        (works[0], steps - 2, swap_send.at[0, 0]),
        (works[1] & (parity == 0), full, swap_send.at[0, 1]),
        (works[1] & (parity == 1), full, swap_send.at[0, 2]),
    ):
        pl.when(mine)(lambda count=count, sem=sem: gone(count - 1, sem))
        pl.when(~mine)(lambda count=count, sem=sem: gone(count, sem))
    for slot in range(2):
        pl.when(works[slot])(lambda slot=slot: gone(steps - 1, swap_send.at[1, slot]))


def local(video, norm_gain, first, second, attn_gain, query_w, key_w, value_w, out_w):
    steps, blocks = (lax.axis_size("tm"), lax.axis_size("rows"))
    frames, height, width, chans = video.shape
    anywhere = pl.BlockSpec(memory_space=pl.ANY)
    square = (chans, chans)
    return pl.pallas_call(
        functools.partial(kernel, steps, blocks),
        out_shape=pltpu.VMEM(video.shape, BF16),
        in_specs=[anywhere] * 9,
        out_specs=pl.BlockSpec(memory_space=pltpu.VMEM),
        scratch_shapes=[
            pltpu.VMEM(video.shape, BF16),
            pltpu.VMEM((1, chans), BF16),
            pltpu.VMEM((3, 3, 3) + square, BF16),
            pltpu.VMEM((3, 3, 3) + square, BF16),
            pltpu.VMEM((1, chans), BF16),
            pltpu.VMEM(square, BF16),
            pltpu.VMEM(square, BF16),
            pltpu.VMEM(square, BF16),
            pltpu.VMEM(square, BF16),
            pltpu.VMEM((4, 8, COLS, chans), BF16),
            pltpu.VMEM((4, 8, COLS, chans), BF16),
            pltpu.VMEM((2, 4, COLS, 3 * chans), F32),
            pltpu.VMEM((4, PER_ROW, 2 * UNIT, chans), BF16),
            pltpu.VMEM((2, steps, 2 * UNIT, chans), BF16),
            pltpu.VMEM((2, steps, 2 * UNIT, chans), BF16),
            pltpu.VMEM((4, PER_ROW, 2 * UNIT, chans), BF16),
            pltpu.SemaphoreType.DMA((9,)),
            pltpu.SemaphoreType.DMA((2, 10)),
            pltpu.SemaphoreType.DMA((2, 10)),
            pltpu.SemaphoreType.DMA((2, 3)),
            pltpu.SemaphoreType.DMA((2, 3)),
        ],
        compiler_params=pltpu.CompilerParams(
            collective_id=0, has_side_effects=True, vmem_limit_bytes=56 * 1024 * 1024
        ),
    )(
        video,
        norm_gain.reshape(1, chans),
        first,
        second,
        attn_gain.reshape(1, chans),
        query_w,
        key_w,
        value_w,
        out_w,
    )


def solution(mesh):
    return jax.shard_map(
        local,
        mesh=mesh,
        in_specs=(P("tm", "rows", None, None), P(), P(), P(), P(), P(), P(), P(), P()),
        out_specs=P("tm", "rows", None, None),
        check_vma=False,
    )
```

```python
import functools

import jax
import jax.numpy as jnp
from jax import lax
from jax.experimental import pallas as pl
from jax.experimental.pallas import tpu as pltpu
from jax.sharding import PartitionSpec as P

F32 = jnp.float32
BF16 = jnp.bfloat16
MESH = pl.DeviceIdType.MESH
COLS = 128
UNIT = 8
PER_ROW = COLS // UNIT


def rms_norm(wide, gain):
    scale = lax.rsqrt(jnp.mean(wide * wide, axis=-1, keepdims=True) + 1e-06)
    return wide * scale * gain


def silu(v):
    return v / (1.0 + jnp.exp(-v))


def column_sum(total):
    width, chans = (COLS - UNIT, total.shape[1] // 3)
    left = pltpu.roll(total[:, :chans], 1, 0)
    right = pltpu.roll(total[:, 2 * chans :], COLS - 1, 0)
    return (left + total[:, chans : 2 * chans] + right)[:width]


def padded(value):
    return jnp.concatenate([value, jnp.zeros((COLS - value.shape[0], value.shape[1]), F32)], axis=0)


def kernel(
    steps,
    blocks,
    video_hbm,
    norm_gain_hbm,
    first_hbm,
    second_hbm,
    attn_gain_hbm,
    query_hbm,
    key_hbm,
    value_hbm,
    out_hbm,
    result_ref,
    video,
    norm_gain,
    first,
    second,
    attn_gain,
    query_w,
    key_w,
    value_w,
    out_w,
    act,
    mid,
    acc,
    hidden,
    gathered,
    answer,
    returned,
    load_sem,
    halo_send,
    halo_recv,
    swap_send,
    swap_recv,
    round_sem,
):
    t, r = (lax.axis_index("tm"), lax.axis_index("rows"))
    chans = video.shape[-1]
    loads = [
        pltpu.make_async_copy(src, dst, load_sem.at[i])
        for i, (src, dst) in enumerate(
            [
                (video_hbm, video),
                (norm_gain_hbm, norm_gain),
                (first_hbm, first),
                (second_hbm, second),
                (attn_gain_hbm, attn_gain),
                (query_hbm, query_w),
                (key_hbm, key_w),
                (value_hbm, value_w),
                (out_hbm, out_w),
            ]
        )
    ]
    for load in loads:
        load.start()

    has_next, has_prev = (t < steps - 1, t > 0)
    has_above, has_below = (r < blocks - 1, r > 0)

    barrier = pltpu.get_barrier_semaphore()

    def partner(k):
        return t + 2**k - 2 ** (k + 1) * lax.rem(t // 2**k, 2)

    beside = t - 1 + 2 * lax.rem(t, 2)
    has_beside = (beside >= 0) & (beside < steps)
    rounds = steps.bit_length() - 1
    for k in range(rounds):
        pl.semaphore_signal(
            barrier, inc=1, device_id={"tm": partner(k), "rows": r}, device_id_type=MESH
        )
    met = rounds + has_beside.astype(jnp.int32)

    @pl.when(has_beside)
    def _():
        pl.semaphore_signal(barrier, inc=1, device_id={"tm": beside, "rows": r}, device_id_type=MESH)

    for side, there in ((1, has_above), (-1, has_below)):
        for shift, then in ((0, True), (1, has_next), (-1, has_prev)):
            present = there if shift == 0 else there & then
            peer = {"tm": t + shift, "rows": r + side}
            met = met + present.astype(jnp.int32)

            @pl.when(present)
            def _(peer=peer):
                pl.semaphore_signal(barrier, inc=1, device_id=peer, device_id_type=MESH)

    flip = (lax.rem(r, 4) < 2).astype(jnp.int32)

    def place(q):
        return q + flip * (3 - 2 * q)

    def line(q):
        return q + 2 + flip * (3 - 2 * q)

    def tap(b):
        return b + flip * (2 - 2 * b)

    for field in (act, mid):

        @pl.when(t == 0)
        def _(field=field):
            field[0:2] = jnp.zeros((2,) + field.shape[1:], BF16)

        @pl.when(r == 0)
        def _(field=field):
            for frame in range(4):
                field[frame, 1] = jnp.zeros((COLS, chans), BF16)

        @pl.when(r == blocks - 1)
        def _(field=field):
            for frame in range(4):
                field[frame, 6] = jnp.zeros((COLS, chans), BF16)

    loads[0].wait()
    loads[1].wait()
    gain = norm_gain[...].astype(F32)
    for frame in range(2):
        for row in range(4):
            wide = video[frame, row].astype(F32)
            act[frame + 2, row + 2] = padded(silu(rms_norm(wide, gain))).astype(BF16)

    pl.semaphore_wait(barrier, met)

    def tell(k):
        pl.semaphore_signal(
            round_sem.at[k], inc=1, device_id={"tm": partner(k), "rows": r}, device_id_type=MESH
        )

    def told(k):
        pl.semaphore_wait(round_sem.at[k], 1)

    def halo(which, field, slots, src, dst, device):
        return pltpu.make_async_remote_copy(
            src_ref=field.at[src],
            dst_ref=field.at[dst],
            send_sem=halo_send.at[which, slots[0]],
            recv_sem=halo_recv.at[which, slots[1]],
            device_id=device,
            device_id_type=MESH,
        )

    own, past = (pl.ds(2, 2), pl.ds(0, 2))
    has_far = jnp.where(flip == 1, has_below, has_above)
    slow = has_far & ((lax.rem(r, 4) == 0) | (lax.rem(r, 4) == 3))
    fast = has_far & ~((lax.rem(r, 4) == 0) | (lax.rem(r, 4) == 3))

    def copies(which, field):
        next_t = jnp.minimum(t + 1, steps - 1)
        near_r = jnp.clip(r - 1 + 2 * flip, 0, blocks - 1)
        far_r = jnp.clip(r + 1 - 2 * flip, 0, blocks - 1)
        later, near, far, next_near, next_far = (
            {"tm": a, "rows": b}
            for a, b in ((next_t, r), (t, near_r), (t, far_r), (next_t, near_r), (next_t, far_r))
        )
        near_land, far_land = (6 - 5 * flip, 1 + 5 * flip)
        far_in = line(4)
        inner = pl.ds(3, 2)
        return {
            "inner": halo(which, field, (0, 0), (own, inner), (past, inner), later),
            "first": halo(which, field, (1, 1), (own, line(0)), (past, line(0)), later),
            "last": halo(which, field, (2, 2), (own, line(3)), (past, line(3)), later),
            "to_near": halo(which, field, (3, 4 - flip), (own, line(0)), (own, near_land), near),
            "to_far": halo(which, field, (4, 3 + flip), (own, line(3)), (own, far_land), far),
            "diag_near": halo(
                which, field, (5, 6 - flip), (own, line(0)), (past, near_land), next_near
            ),
            "diag_far": halo(
                which, field, (6, 5 + flip), (own, line(3)), (past, far_land), next_far
            ),
            "from_near": halo(which, field, (3, 3 + flip), (own, line(0)), (own, line(-1)), near),
            "from_far": halo(which, field, (4, 4 - flip), (own, line(3)), (own, far_in), far),
            "past_near": halo(which, field, (5, 5 + flip), (own, line(0)), (past, line(-1)), later),
            "on_far": halo(which, field, (7, 6 - flip), (own, far_in), (past, far_in), later),
        }

    def when(flag, action):
        pl.when(flag)(action)

    def product(field, weight, frame, early, rows, span):
        pairs = [(a, b) for a in early for b in span]
        cells = jnp.concatenate(
            [
                jnp.concatenate([field[frame + a, line(q + b - 1)] for q in rows], axis=0)
                for a, b in pairs
            ],
            axis=1,
        )
        taps = jnp.concatenate(
            [
                jnp.concatenate([weight[a, tap(b), e] for e in range(3)], axis=1)
                for a, b in pairs
            ],
            axis=0,
        )
        return jnp.dot(cells, taps, preferred_element_type=F32)

    def part(total, i):
        return total[i * COLS : (i + 1) * COLS]

    every = (0, 1, 2)
    groups = (((1, 2), every), ((0,), (1, 2)), ((3,), (0, 1)))

    def to_mid(frame, q, total):
        mid[frame + 2, line(q)] = padded(silu(column_sum(total))).astype(BF16)

    def to_hidden(q, totals):
        one, two = (
            padded(video[frame, place(q)].astype(F32) + column_sum(total)).reshape(
                PER_ROW, UNIT, chans
            )
            for frame, total in enumerate(totals)
        )
        hidden[q] = jnp.concatenate([one, two], axis=1).astype(BF16)

    parity = lax.rem(t, 2)
    full = PER_ROW - 1
    works = [lax.rem(t, PER_ROW) < full, t // 2 < full]

    def peer_copy(src, dst, send, recv, peer):
        return pltpu.make_async_remote_copy(
            src_ref=src,
            dst_ref=dst,
            send_sem=send,
            recv_sem=recv,
            device_id={"tm": peer, "rows": r},
            device_id_type=MESH,
        )

    def scatter_all():
        def body(j, _):
            peer = lax.rem(t + j, steps)
            copy = peer_copy(
                hidden.at[peer // PER_ROW, lax.rem(peer, PER_ROW)],
                gathered.at[0, t],
                swap_send.at[0, 0],
                swap_recv.at[0, 0],
                peer,
            )
            pl.when(lax.rem(peer, PER_ROW) < full)(copy.start)
            return 0

        lax.fori_loop(1, steps, body, 0)
        own_unit = pltpu.make_async_copy(
            hidden.at[t // PER_ROW, lax.rem(t, PER_ROW)], gathered.at[0, t], swap_recv.at[0, 0]
        )
        pl.when(works[0])(own_unit.start)

    def scatter_half(odd):
        def send(j):
            spot = lax.rem(t // 2 + j, PER_ROW)
            copy = peer_copy(
                hidden.at[2 + odd, spot],
                gathered.at[1, t],
                swap_send.at[0, 1 + odd],
                swap_recv.at[0, 1],
                2 * spot + odd,
            )
            pl.when(spot < full)(copy.start)

        def body(j, _):
            send(j)
            return 0

        lax.fori_loop(1, PER_ROW, body, 0)
        pl.when(parity != odd)(lambda: send(0))
        pl.when((parity == odd) & works[1])(
            pltpu.make_async_copy(
                hidden.at[2 + odd, t // 2], gathered.at[1, t], swap_recv.at[0, 1]
            ).start
        )

    def attend(slot):
        pltpu.make_async_copy(gathered.at[slot], gathered.at[slot], swap_recv.at[0, slot]).wait()
        cells = steps * 2 * UNIT
        wide = gathered[slot].reshape(cells, chans).astype(F32)
        normed = rms_norm(wide, attn_gain[...].astype(F32)).astype(BF16)
        joined = jnp.concatenate([query_w[...], key_w[...], value_w[...]], axis=1)
        projected = jnp.dot(normed, joined, preferred_element_type=F32).astype(BF16)
        query = projected[:, :chans]
        key = projected[:, chans : 2 * chans]
        value = projected[:, 2 * chans :]
        tile = 128
        spot = lax.broadcasted_iota(jnp.int32, (tile, tile), 0)
        other = lax.broadcasted_iota(jnp.int32, (tile, tile), 1)
        same = lax.rem(spot, UNIT) == lax.rem(other, UNIT)
        causal = same & (other <= spot)
        root = 1.0 / jnp.sqrt(F32(chans))
        for i in range(cells // tile):
            rows = slice(i * tile, (i + 1) * tile)
            scores = (
                lax.dot_general(
                    query[rows],
                    key[: (i + 1) * tile],
                    (((1,), (1,)), ((), ())),
                    preferred_element_type=F32,
                )
                * root
            )
            tiles = [
                jnp.where(
                    causal if j == i else same, scores[:, j * tile : (j + 1) * tile], F32(-1e30)
                )
                for j in range(i + 1)
            ]
            top = jnp.max(functools.reduce(jnp.maximum, tiles), axis=1, keepdims=True)
            weights = [jnp.exp(one - top) for one in tiles]
            total = jnp.sum(functools.reduce(jnp.add, weights), axis=1, keepdims=True)
            mixed = jnp.dot(
                jnp.concatenate([one.astype(BF16) for one in weights], axis=1),
                value[: (i + 1) * tile],
                preferred_element_type=F32,
            )
            mixed = (mixed / total).astype(BF16)
            shown = wide[rows] + jnp.dot(mixed, out_w[...], preferred_element_type=F32)
            count = tile // (2 * UNIT)
            answer[slot, i * count : (i + 1) * count] = shown.astype(BF16).reshape(
                count, 2 * UNIT, chans
            )
        if slot == 0:
            home = returned.at[t // PER_ROW, lax.rem(t, PER_ROW)]
            arrived = swap_recv.at[1, 0]
        else:
            home = returned.at[2 + parity, t // 2]
            arrived = swap_recv.at[1, 1 + parity]

        def body(j, _):
            peer = lax.rem(t + j, steps)
            peer_copy(answer.at[slot, peer], home, swap_send.at[1, slot], arrived, peer).start()
            return 0

        lax.fori_loop(1, steps, body, 0)
        pltpu.make_async_copy(answer.at[slot, t], home, arrived).start()

    def collect(index, rows):
        block = returned.at[pl.ds(rows[0], len(rows)), pl.ds(0, full)]
        pltpu.make_async_copy(block, block, swap_recv.at[1, index]).wait()
        for q in rows:
            units = returned[q, 0:full].astype(F32)
            for frame in range(2):
                cols = units[:, frame * UNIT : (frame + 1) * UNIT].reshape(full * UNIT, chans)
                result_ref[frame, place(q)] = cols.astype(BF16)

    one, two = (copies(0, act), copies(1, mid))
    when(has_far, one["to_far"].start)
    one["to_near"].start()
    when(has_next, one["diag_near"].start)
    when(has_next & fast, one["diag_far"].start)
    for name in ("inner", "first", "last"):
        when(has_next, one[name].start)
    tell(0)
    loads[2].wait()
    for frame in range(2):
        for rows, span in groups:
            total = product(act, first, frame, range(2 - frame, 3), rows, span)
            for i, q in enumerate(rows):
                acc[frame, q] = part(total, i)
    told(0)
    tell(1)
    for name in ("inner", "first", "last"):
        when(has_prev, one[name].wait_recv)
    for rows, span in groups:
        for frame in range(2):
            total = product(act, first, frame, range(0, 2 - frame), rows, span)
            for i, q in enumerate(rows):
                if len(rows) == 2:
                    to_mid(frame, q, acc[frame, q] + part(total, i))
                else:
                    acc[frame, q] += part(total, i)
        if len(rows) == 2:
            when(has_next, two["inner"].start)

    def edge(field, weight, q):
        return [
            acc[frame, q] + product(field, weight, frame, every, (q,), (0,) if q == 0 else (2,))
            for frame in range(2)
        ]

    told(1)
    tell(2)
    one["from_near"].wait_recv()
    when(has_prev, one["past_near"].wait_recv)
    for frame, total in enumerate(edge(act, first, 0)):
        to_mid(frame, 0, total)
    two["to_near"].start()
    when(has_next, two["diag_near"].start)
    when(has_next, two["first"].start)
    told(2)
    tell(3)
    when(has_far, one["from_far"].wait_recv)
    when(has_next & slow, one["on_far"].start)
    when(has_prev & has_far, one["on_far"].wait_recv)
    for frame, total in enumerate(edge(act, first, 3)):
        to_mid(frame, 3, total)
    when(has_far, two["to_far"].start)
    when(has_next & fast, two["diag_far"].start)
    when(has_next, two["last"].start)

    told(3)
    tell(4)
    loads[3].wait()
    for name in ("inner", "first"):
        when(has_prev, two[name].wait_recv)
    to_hidden(1, [product(mid, second, frame, every, (1,), every) for frame in range(2)])
    for frame in range(2):
        acc[frame, 0] = product(mid, second, frame, every, (0,), (1, 2))
    two["from_near"].wait_recv()
    when(has_prev, two["past_near"].wait_recv)
    to_hidden(0, edge(mid, second, 0))
    told(4)
    scatter_all()

    when(has_prev, two["last"].wait_recv)
    to_hidden(2, [product(mid, second, frame, every, (2,), every) for frame in range(2)])
    scatter_half(0)
    for frame in range(2):
        acc[frame, 3] = product(mid, second, frame, every, (3,), (0, 1))
    when(has_far, two["from_far"].wait_recv)
    when(has_next & slow, two["on_far"].start)
    when(has_prev & has_far, two["on_far"].wait_recv)
    to_hidden(3, edge(mid, second, 3))
    scatter_half(1)

    for load in loads[4:]:
        load.wait()
    for slot in range(2):
        pl.when(works[slot])(lambda slot=slot: attend(slot))
    collect(0, (0, 1))
    collect(1, (2,))
    collect(2, (3,))

    for copy in (one, two):
        copy["to_near"].wait_send()
        for name in ("inner", "first", "last", "diag_near"):
            when(has_next, copy[name].wait_send)
        when(has_next & fast, copy["diag_far"].wait_send)
    for copy in (one, two):
        when(has_far, copy["to_far"].wait_send)
        when(has_next & slow, copy["on_far"].wait_send)

    def gone(count, sem):
        sent = gathered.at[0, pl.ds(0, count)]
        pltpu.make_async_copy(sent, sent, sem).wait()

    for mine, count, sem in (
        (works[0], steps - 2, swap_send.at[0, 0]),
        (works[1] & (parity == 0), full, swap_send.at[0, 1]),
        (works[1] & (parity == 1), full, swap_send.at[0, 2]),
    ):
        pl.when(mine)(lambda count=count, sem=sem: gone(count - 1, sem))
        pl.when(~mine)(lambda count=count, sem=sem: gone(count, sem))
    for slot in range(2):
        pl.when(works[slot])(lambda slot=slot: gone(steps - 1, swap_send.at[1, slot]))


def local(video, norm_gain, first, second, attn_gain, query_w, key_w, value_w, out_w):
    steps, blocks = (lax.axis_size("tm"), lax.axis_size("rows"))
    frames, height, width, chans = video.shape
    anywhere = pl.BlockSpec(memory_space=pl.ANY)
    square = (chans, chans)
    return pl.pallas_call(
        functools.partial(kernel, steps, blocks),
        out_shape=pltpu.VMEM(video.shape, BF16),
        in_specs=[anywhere] * 9,
        out_specs=pl.BlockSpec(memory_space=pltpu.VMEM),
        scratch_shapes=[
            pltpu.VMEM(video.shape, BF16),
            pltpu.VMEM((1, chans), BF16),
            pltpu.VMEM((3, 3, 3) + square, BF16),
            pltpu.VMEM((3, 3, 3) + square, BF16),
            pltpu.VMEM((1, chans), BF16),
            pltpu.VMEM(square, BF16),
            pltpu.VMEM(square, BF16),
            pltpu.VMEM(square, BF16),
            pltpu.VMEM(square, BF16),
            pltpu.VMEM((4, 8, COLS, chans), BF16),
            pltpu.VMEM((4, 8, COLS, chans), BF16),
            pltpu.VMEM((2, 4, COLS, 3 * chans), F32),
            pltpu.VMEM((4, PER_ROW, 2 * UNIT, chans), BF16),
            pltpu.VMEM((2, steps, 2 * UNIT, chans), BF16),
            pltpu.VMEM((2, steps, 2 * UNIT, chans), BF16),
            pltpu.VMEM((4, PER_ROW, 2 * UNIT, chans), BF16),
            pltpu.SemaphoreType.DMA((9,)),
            pltpu.SemaphoreType.DMA((2, 10)),
            pltpu.SemaphoreType.DMA((2, 10)),
            pltpu.SemaphoreType.DMA((2, 3)),
            pltpu.SemaphoreType.DMA((2, 3)),
            pltpu.SemaphoreType.REGULAR((5,)),
        ],
        compiler_params=pltpu.CompilerParams(
            collective_id=0, has_side_effects=True, vmem_limit_bytes=56 * 1024 * 1024
        ),
    )(
        video,
        norm_gain.reshape(1, chans),
        first,
        second,
        attn_gain.reshape(1, chans),
        query_w,
        key_w,
        value_w,
        out_w,
    )


def solution(mesh):
    return jax.shard_map(
        local,
        mesh=mesh,
        in_specs=(P("tm", "rows", None, None), P(), P(), P(), P(), P(), P(), P(), P()),
        out_specs=P("tm", "rows", None, None),
        check_vma=False,
    )
```
